256 devices in a mesh: pipe: 4 (over x), expert: 64 (over z, y, core).
Axes of the slice: x: 4, y: 4, z: 8, core: 2. Of those that a mesh axis runs over, the one named last changes fastest.
Arguments:
- cotangent: bfloat16 [2, 4096, 1024], P(None, 'expert'), may hold values from -6 to 6
- expert_ids: int32 [4, 2, 4096, 6], P('pipe', None, 'expert'), may hold values from 0 to 63, all different within a row; in each aligned block of 64 rows (0 to 63, 64 to 127, ..., all dimensions but the last counted through in order) at most 7 rows name the same one
- gates: float32 [4, 2, 4096, 6], P('pipe', None, 'expert'), may hold values from 0.03 to 0.5
- layer_inputs: bfloat16 [4, 2, 4096, 1024], P('pipe', None, 'expert'), may hold values from -3 to 3
- saved_fc1: bfloat16 [4, 2, 64, 448, 1408], P('pipe', None, 'expert'), may hold values from -6 to 6
- w_fc1: bfloat16 [4, 64, 1024, 1408], P('pipe', 'expert'), may hold values from -0.1875 to 0.1875
- w_fc2: bfloat16 [4, 64, 704, 1024], P('pipe', 'expert'), may hold values from -0.21875 to 0.21875
Outputs:
- section_grads: bfloat16 [4, 2, 4096, 1024], P('pipe', None, 'expert')
- fc1_grad: bfloat16 [4, 64, 1024, 1408], P('pipe', 'expert')
- fc2_grad: bfloat16 [4, 64, 704, 1024], P('pipe', 'expert')
The draws below stay inside these ranges and needn't reach their ends.
Inputs may be any that keep to these rules, and one draw needn't show every extreme that they name: `expert_ids`: each token names 6 different experts; in each section, micro-batch and aligned block of 64 tokens no expert is named by more than 7 tokens.
All inputs are finite; a program needn't handle non-finite values.
Results may differ from the reference program's by a relative error of at most 0.015.
Values may be sent and summed in bfloat16 or wider, within the bound.
A program may use at most 128 MiB of HBM per device.

```python
import math
import jax
import jax.numpy as jnp
import numpy as np
from jax import lax

D = 1024
FFW = 704
TOP = 6
MB = 2
TOK_DEV = 64
SECTIONS = 4
EXPERTS = 64
TOKENS = 4096
CAP = 7
SLOTS = 448
N_EXPERT = 64


def block_scale(key, extent, shards, least, largest):
    def one(position, blocks):
        draws = jax.random.uniform(jax.random.fold_in(jax.random.fold_in(key, 6), position), (blocks,), jnp.float32, least / len(shards), largest / len(shards))
        return jnp.repeat(jnp.exp(draws), extent[position] // blocks).reshape((-1,) + (1,) * (len(extent) - position - 1))

    loudness = one(*shards[0])
    for cut in shards[1:]:
        loudness = loudness * one(*cut)
    return loudness


def routed_block(stream_key, own, number, rows, count, top, limit, lean):
    ranking = jax.random.permutation(stream_key, count)
    heavy_load, common = portions_of(count, rows * top, limit, lean, True), portions_of(count, rows * top, limit, lean, False)
    places = jnp.arange(count)

    def named(sizes, turn):
        used = int((sizes > 0).sum())
        fixed = max(1, used // 4)
        passed = fixed + (places - fixed + turn * (used - fixed)) % max(1, count - fixed)
        return jnp.zeros((count,), jnp.int32).at[ranking[jnp.where(places < fixed, places, passed)]].set(jnp.asarray(sizes, jnp.int32))

    sizes = jnp.where(number % 4 == 0, named(heavy_load, number // 4), named(common, number - number // 4 - 1))
    mixed = jax.random.permutation(jax.random.fold_in(own, 3), count)
    giver, taker = mixed[0:count // 2 * 2:2], mixed[1:count // 2 * 2:2]
    margin = jnp.minimum(sizes[giver] - 1, limit - sizes[taker]) // 2
    margin = jnp.where((giver == ranking[0]) | (taker == ranking[0]) | (sizes[taker] == 0), 0, jnp.maximum(margin, 0))
    passed = jax.random.randint(jax.random.fold_in(own, 4), (count // 2,), 0, 1 << 20) % (margin + 1)
    sizes = sizes.at[giver].add(-passed).at[taker].add(passed)
    items = jnp.searchsorted(jnp.cumsum(sizes), jnp.arange(rows * top), side="right").astype(jnp.int32)
    listing = items.reshape(top, rows).T
    listing = listing[jax.random.permutation(jax.random.fold_in(own, 1), rows)]
    turn = jax.random.randint(jax.random.fold_in(own, 2), (rows, 1), 0, top)
    return jnp.take_along_axis(listing, (jnp.arange(top)[None, :] + turn) % top, axis=1)


def portions_of(amount, total, limit, skew, full):
    weights = [(1 << 20) // math.isqrt(standing ** skew) + 1 for standing in range(1, amount + 1)]
    largest = limit if full else min(limit, max(-(-total // amount), total * weights[0] // sum(weights)))
    least = 1 if total - largest >= amount - 1 else 0
    given, surplus = [largest] + [least] * (amount - 1), total - largest - least * (amount - 1)
    while surplus > 0:
        free = [i for i in range(1, amount) if given[i] < largest] or [i for i in range(1, amount) if given[i] < limit]
        pool, budget = sum([weights[i] for i in free]), surplus
        for i in free:
            more = min(limit - given[i], max(1, budget * weights[i] // pool), surplus)
            given[i] = given[i] + more
            surplus = surplus - more
    return np.array(given)


def centred(key, extent, scale, bound, pieces=(), kind=jnp.bfloat16):
    values = scale * jax.random.normal(key, extent, jnp.float32)
    if pieces:
        values = values * block_scale(key, extent, pieces, -0.22, 0.18)
    return jnp.clip(values, -bound, bound).astype(kind)


def setup_inputs(seed: int = 0) -> dict:
    splits = jax.random.split(jax.random.key(seed), 8)
    cotangent = centred(splits[0], (MB, TOKENS, D), 1.0, 6.0, ((1, 64),))
    expert_ids_keys = jax.random.split(jax.random.fold_in(splits[1], 1), SECTIONS * MB * TOKENS // TOK_DEV)
    expert_ids_turns = jax.random.permutation(jax.random.fold_in(splits[1], 3), SECTIONS * MB * TOKENS // TOK_DEV)
    expert_ids = jax.vmap(lambda own, number: routed_block(jax.random.fold_in(splits[1], 2), own, number, TOK_DEV, EXPERTS, TOP, CAP, 2))(expert_ids_keys, expert_ids_turns).reshape((SECTIONS, MB, TOKENS, TOP))
    gates = jnp.clip(jnp.exp(math.log(0.5) - 2.8134107 * jax.random.uniform(splits[2], (SECTIONS, MB, TOKENS, TOP), jnp.float32) ** block_scale(splits[2], (SECTIONS, MB, TOKENS, TOP), ((0, 4), (2, 64)), -0.2, 0.2)), 0.03, 0.5)
    layer_inputs = centred(splits[3], (SECTIONS, MB, TOKENS, D), 0.5, 3.0, ((0, 4), (2, 64)))
    saved_fc1 = centred(splits[4], (SECTIONS, MB, EXPERTS, SLOTS, 2 * FFW), 1.0, 6.0, ((0, 4), (2, 64)))
    w_fc1 = centred(splits[5], (SECTIONS, EXPERTS, D, 2 * FFW), D ** -0.5, 0.1875, ((0, 4), (1, 64)))
    w_fc2 = centred(splits[6], (SECTIONS, EXPERTS, FFW, D), FFW ** -0.5, 0.21875, ((0, 4), (1, 64)))
    return dict(cotangent=cotangent, expert_ids=expert_ids, gates=gates, layer_inputs=layer_inputs, saved_fc1=saved_fc1, w_fc1=w_fc1, w_fc2=w_fc2)


def slot_targets(expert_now):
    blocked = expert_now.reshape(N_EXPERT, TOK_DEV * TOP)
    onehot = (blocked[:, :, None] == jnp.arange(EXPERTS, dtype=jnp.int32)[None, None, :]).astype(jnp.int32)
    earlier = (jnp.cumsum(onehot, axis=1) - onehot).astype(jnp.int32)
    slot_index = jnp.sum(earlier * onehot, axis=2).astype(jnp.int32)
    sources = jnp.arange(N_EXPERT, dtype=jnp.int32)[:, None]
    return ((blocked * N_EXPERT + sources) * CAP + slot_index).reshape(-1).astype(jnp.int32)


def expert_grads(routed, fc1_now, weight_one, weight_two):
    hidden_width = weight_two.shape[0]
    hidden_grad = lax.dot_general(routed, weight_two, (((1,), (1,)), ((), ())), preferred_element_type=jnp.float32)
    pre_gate = fc1_now[:, :hidden_width].astype(jnp.float32)
    pre_up = fc1_now[:, hidden_width:].astype(jnp.float32)
    sigmoid_v = jax.nn.sigmoid(pre_gate)
    gate_part = (hidden_grad * pre_up * (sigmoid_v * (1.0 + pre_gate * (1.0 - sigmoid_v)))).astype(jnp.bfloat16)
    up_part = (hidden_grad * (pre_gate * sigmoid_v)).astype(jnp.bfloat16)
    fc1_out_grad = jnp.concatenate([gate_part, up_part], axis=1)
    row_grads = lax.dot_general(fc1_out_grad, weight_one, (((1,), (1,)), ((), ())), preferred_element_type=jnp.float32)
    return fc1_out_grad, row_grads.astype(jnp.bfloat16)


def weight_terms(fc1_now, routed, routed_x, fc1_out_grad):
    hidden_width = fc1_now.shape[1] // 2
    pre_gate = fc1_now[:, :hidden_width].astype(jnp.float32)
    pre_up = fc1_now[:, hidden_width:].astype(jnp.float32)
    activation = (pre_gate * jax.nn.sigmoid(pre_gate) * pre_up).astype(jnp.bfloat16)
    term_two = lax.dot_general(activation, routed, (((0,), (0,)), ((), ())), preferred_element_type=jnp.float32)
    term_one = lax.dot_general(routed_x, fc1_out_grad, (((0,), (0,)), ((), ())), preferred_element_type=jnp.float32)
    return term_one, term_two


def reference(cotangent, expert_ids, gates, layer_inputs, saved_fc1, w_fc1, w_fc2):
    grad_now = cotangent
    section_list = []
    fc1_list = []
    fc2_list = []
    for section_no in range(SECTIONS - 1, -1, -1):
        outputs = []
        acc_one = jnp.zeros((EXPERTS, D, 2 * FFW), jnp.float32)
        acc_two = jnp.zeros((EXPERTS, FFW, D), jnp.float32)
        for micro_no in range(MB):
            target = slot_targets(expert_ids[section_no, micro_no])
            grad_in = grad_now[micro_no]
            scaled = (gates[section_no, micro_no][:, :, None] * grad_in[:, None, :].astype(jnp.float32)).astype(jnp.bfloat16)
            routed = jnp.zeros((EXPERTS * SLOTS, D), jnp.bfloat16).at[target].set(scaled.reshape(-1, D)).reshape(EXPERTS, SLOTS, D)
            token_rows = jnp.broadcast_to(layer_inputs[section_no, micro_no][:, None, :], (TOKENS, TOP, D)).reshape(-1, D)
            routed_x = jnp.zeros((EXPERTS * SLOTS, D), jnp.bfloat16).at[target].set(token_rows).reshape(EXPERTS, SLOTS, D)
            fc1_out_grad, row_grads = lax.map(lambda args: expert_grads(*args), (routed, saved_fc1[section_no, micro_no], w_fc1[section_no], w_fc2[section_no]))
            picked = row_grads.reshape(-1, D)[target].reshape(TOKENS, TOP, D).astype(jnp.float32)
            outputs.append((grad_in.astype(jnp.float32) + jnp.sum(picked, axis=1)).astype(jnp.bfloat16))
            term_one, term_two = lax.map(lambda args: weight_terms(*args), (saved_fc1[section_no, micro_no], routed, routed_x, fc1_out_grad))
            acc_one = acc_one + term_one
            acc_two = acc_two + term_two
        grad_now = jnp.stack(outputs)
        section_list.append(grad_now)
        fc1_list.append(acc_one.astype(jnp.bfloat16))
        fc2_list.append(acc_two.astype(jnp.bfloat16))
    section_grads = jnp.stack(section_list[::-1])
    fc1_grad = jnp.stack(fc1_list[::-1])
    fc2_grad = jnp.stack(fc2_list[::-1])
    return section_grads, fc1_grad, fc2_grad
```

```python
import functools

import jax
import jax.numpy as jnp
from jax import lax
from jax.experimental import pallas as pl
from jax.experimental.pallas import tpu as pltpu
from jax.sharding import PartitionSpec as P

MESH = pl.DeviceIdType.MESH
NZ = 8
PAD = 8
RIGHT, LEFT = 0, 1
F32, BF16 = jnp.float32, jnp.bfloat16


def block_of(direction, step):
    if step == 0:
        return 0
    if step == 4:
        return 7
    return 2 * step - 1 if direction == RIGHT else 2 * step


def streams(step):
    if step == 4:
        return ((0, RIGHT), (1, LEFT))
    return tuple((half, direction) for half in (0, 1) for direction in (RIGHT, LEFT))


def fused_kernel(
    dims,
    cot,
    smat,
    xin,
    saved_hbm,
    w1_hbm,
    w2_hbm,
    sec_out,
    g1_out,
    g2_out,
    gath,
    sendb,
    routed,
    rsend,
    rrecv,
    part,
    ring_send,
    ring_recv,
    gout,
    srecv,
    sel,
    comb,
    w1v,
    w2d,
    savedv,
    factor,
    act,
    fog,
    z_send,
    z_recv,
    y_send,
    y_recv,
    r_send,
    r_recv,
    q_send,
    q_recv,
    x_send,
    x_recv,
    s_send,
    s_recv,
    local_sem,
    own_sem,
):
    sections, nyc, tok, width, wide, cap = dims
    hidden = wide // 2
    half_cols = width // 2
    rows_in = NZ * nyc * cap
    rows = NZ * nyc * PAD
    per_peer = NZ * PAD
    pair_rows = 2 * nyc * PAD
    sel_rows = nyc * PAD

    pipe = lax.axis_index("pipe")
    expert = lax.axis_index("expert")
    zi = expert // nyc
    me = expert % nyc

    def along_z(by):
        return (pipe, ((zi + by) % NZ) * nyc + me)

    def along_y(yc):
        return (pipe, zi * nyc + yc)

    right, left = along_z(1), along_z(NZ - 1)
    x_next = ((pipe + sections - 1) % sections, expert)
    x_prev = ((pipe + 1) % sections, expert)

    weight_copies = (
        pltpu.make_async_copy(w1_hbm, w1v, local_sem.at[0]),
        pltpu.make_async_copy(w2_hbm, w2d.at[pl.ds(0, hidden), :], local_sem.at[1]),
        pltpu.make_async_copy(w2_hbm, w2d.at[pl.ds(hidden, hidden), :], local_sem.at[2]),
        pltpu.make_async_copy(saved_hbm.at[0], savedv.at[0, pl.ds(0, rows_in), :], local_sem.at[3]),
        pltpu.make_async_copy(saved_hbm.at[1], savedv.at[1, pl.ds(0, rows_in), :], local_sem.at[4]),
    )

    barrier = pltpu.get_barrier_semaphore()
    for by in range(1, NZ):
        pl.semaphore_signal(barrier, inc=1, device_id=along_z(by), device_id_type=MESH)
    for by in range(1, nyc):
        pl.semaphore_signal(
            barrier, inc=1, device_id=along_y((me + by) % nyc), device_id_type=MESH
        )
    pl.semaphore_signal(barrier, inc=1, device_id=x_next, device_id_type=MESH)
    pl.semaphore_signal(barrier, inc=1, device_id=x_prev, device_id_type=MESH)

    for copy in weight_copies:
        copy.start()
    for mb in range(2):
        gath[2 + mb, 0, 0:tok, :] = xin[mb]
        if rows > rows_in:
            savedv[mb, rows_in:rows, :] = jnp.zeros((rows - rows_in, wide), BF16)

    @pl.when(pipe == sections - 1)
    def _():
        for mb in range(2):
            gath[mb, 0, 0:tok, :] = cot[mb]

    srecv[0] = smat[pl.ds(pl.multiple_of(zi * sel_rows, sel_rows), sel_rows), :]
    pl.semaphore_wait(barrier, NZ + nyc)

    def selection_copy(by):
        at = 2 * by - 1 if by <= 4 else 2 * (NZ - by)
        to = (zi + by) % NZ
        return pltpu.make_async_remote_copy(
            src_ref=smat.at[pl.ds(pl.multiple_of(to * sel_rows, sel_rows), sel_rows), :],
            dst_ref=srecv.at[at],
            send_sem=s_send.at[by],
            recv_sem=s_recv.at[at],
            device_id=along_z(by),
            device_id_type=MESH,
        )

    def block_view(task, at, half):
        return gath.at[
            task, at // 2, pl.ds((at % 2) * tok, tok), pl.ds(half * half_cols, half_cols)
        ]

    def z_copy(task, direction, step, half):
        return pltpu.make_async_remote_copy(
            src_ref=block_view(task, block_of(direction, step - 1), half),
            dst_ref=block_view(task, block_of(direction, step), half),
            send_sem=z_send.at[task, direction, step - 1, half],
            recv_sem=z_recv.at[task, direction, step - 1, half],
            device_id=right if direction == RIGHT else left,
            device_id_type=MESH,
        )

    def y_copy(task, by, at, count):
        to = (me + by) % nyc
        return pltpu.make_async_remote_copy(
            src_ref=sendb.at[task, to, pl.ds(at, count), :],
            dst_ref=routed.at[task, me, pl.ds(at, count), :],
            send_sem=y_send.at[task, by],
            recv_sem=y_recv.at[task, by],
            device_id=along_y(to),
            device_id_type=MESH,
        )

    def y_arrival(task, by):
        of = (me + nyc - by) % nyc
        return pltpu.make_async_remote_copy(
            src_ref=sendb.at[task, of],
            dst_ref=routed.at[task, of],
            send_sem=y_send.at[task, by],
            recv_sem=y_recv.at[task, by],
            device_id=along_y(of),
            device_id_type=MESH,
        )

    def own_copy(task):
        return pltpu.make_async_copy(sendb.at[task, me], routed.at[task, me], own_sem.at[task])

    def r_copy(mb, by):
        to = (me + by) % nyc
        return pltpu.make_async_remote_copy(
            src_ref=rsend.at[mb, to],
            dst_ref=rrecv.at[mb, me],
            send_sem=r_send.at[mb, by],
            recv_sem=r_recv.at[mb, by],
            device_id=along_y(to),
            device_id_type=MESH,
        )

    def r_arrival(mb, by):
        of = (me + nyc - by) % nyc
        return pltpu.make_async_remote_copy(
            src_ref=rsend.at[mb, of],
            dst_ref=rrecv.at[mb, of],
            send_sem=r_send.at[mb, by],
            recv_sem=r_recv.at[mb, by],
            device_id=along_y(of),
            device_id_type=MESH,
        )

    def own_return(mb):
        return pltpu.make_async_copy(rsend.at[mb, me], rrecv.at[mb, me], own_sem.at[4 + mb])

    def q_copy(mb, direction, step, half):
        cols = pl.ds(half * half_cols, half_cols)
        return pltpu.make_async_remote_copy(
            src_ref=ring_send.at[mb, direction, step - 1, :, cols],
            dst_ref=ring_recv.at[mb, direction, step - 1, :, cols],
            send_sem=q_send.at[mb, direction, step - 1, half],
            recv_sem=q_recv.at[mb, direction, step - 1, half],
            device_id=right if direction == RIGHT else left,
            device_id_type=MESH,
        )

    def x_copy(mb, half):
        return pltpu.make_async_remote_copy(
            src_ref=gout.at[mb, :, pl.ds(half * half_cols, half_cols)],
            dst_ref=block_view(mb, 0, half),
            send_sem=x_send.at[mb, half],
            recv_sem=x_recv.at[mb, half],
            device_id=x_next,
            device_id_type=MESH,
        )

    def plan(turn):
        mb = turn - (sections - 1 - pipe)
        is_grad = (mb >= 0) & (mb < 2)
        last = pipe == sections - 1
        before = pipe == sections - 2
        x_turn = jnp.where(last, turn - 2, jnp.where(before, jnp.where(turn == 0, 0, turn - 2), turn))
        is_x = jnp.logical_not(is_grad) & (x_turn >= 0) & (x_turn < 2)
        task = jnp.where(is_grad, mb, 2 + x_turn)
        return mb, is_grad, is_grad | is_x, task

    def ring_start(task):
        for half, direction in streams(1):
            z_copy(task, direction, 1, half).start()

    for by in range(1, NZ):
        selection_copy(by).start()
    ring_start(plan(0)[3])

    lane = lax.broadcasted_iota(jnp.int32, (sel_rows, 2 * tok), 1)
    low = lane < tok
    for by in range(1, NZ):
        selection_copy(by).wait_recv()
    for pair in range(NZ // 2):
        first, second = srecv[2 * pair].astype(F32), srecv[2 * pair + 1].astype(F32)
        for mb in range(2):
            one = first if mb == 0 else pltpu.roll(first, tok, 1)
            two = second if mb == 1 else pltpu.roll(second, tok, 1)
            one = jnp.where(low, one, 0.0)
            two = jnp.where(low, 0.0, two)
            pieces = []
            for yc in range(nyc):
                pieces += [one[yc * PAD : (yc + 1) * PAD], two[yc * PAD : (yc + 1) * PAD]]
            both = jnp.concatenate(pieces, axis=0)
            ones = jnp.where(both != 0.0, 1.0, 0.0)
            sel[mb, pair] = both.astype(BF16)
            sel[2 + mb, pair] = ones.astype(BF16)
            comb[mb, pair] = ones.T.astype(BF16)

    def gather(task):
        for step in range(1, 5):
            for half, direction in streams(step):
                z_copy(task, direction, step, half).wait_recv()
                if step < 4 and (half, direction) in streams(step + 1):
                    z_copy(task, direction, step + 1, half).start()
            pair = step - 1
            chosen = jnp.dot(sel[task, pair], gath[task, pair], preferred_element_type=F32).astype(
                BF16
            )
            at = pair * 2 * PAD
            for yc in range(nyc):
                sendb[task, yc, at : at + 2 * PAD, :] = chosen[
                    yc * 2 * PAD : (yc + 1) * 2 * PAD
                ]
            for by in range(1, nyc):
                y_copy(task, by, at, 2 * PAD).start()
        own_copy(task).start()

    def finish_gather(task):
        for by in range(1, nyc):
            y_arrival(task, by).wait_recv()
        own_copy(task).wait()

    def finish_sends(task):
        for step in range(1, 5):
            for half, direction in streams(step):
                z_copy(task, direction, step, half).wait_send()
        for by in range(1, nyc):
            y_arrival(task, by).wait_send()

    chunk = min(128, rows)

    def factors(mb):
        def body(i, carry):
            at = pl.multiple_of(i * chunk, chunk)
            row = lax.broadcasted_iota(jnp.int32, (chunk, rows), 0) + at
            col = lax.broadcasted_iota(jnp.int32, (chunk, rows), 1)
            yc = row // per_peer
            block = (row // PAD) % NZ
            slot = row % PAD
            rel = jnp.where(block % 2 == 1, NZ - (block + 1) // 2, block // 2)
            zz = (zi + rel) % NZ
            want = zz * (nyc * cap) + yc * cap + slot
            pick = jnp.where((col == want) & (slot < cap), 1.0, 0.0).astype(BF16)
            val = jnp.dot(pick, savedv[mb], preferred_element_type=F32)
            swapped = pltpu.roll(val, hidden, 1)
            is_gate = lax.broadcasted_iota(jnp.int32, (chunk, wide), 1) < hidden
            a = jnp.where(is_gate, val, swapped)
            u = jnp.where(is_gate, swapped, val)
            sg = jax.nn.sigmoid(a)
            silu = a * sg
            factor[mb, pl.ds(at, chunk), :] = jnp.where(
                is_gate, u * (sg * (1.0 + a * (1.0 - sg))), silu
            )
            act[pl.ds(mb * rows + at, chunk), :] = (silu * u)[:, : act.shape[1]].astype(BF16)
            return carry

        lax.fori_loop(0, rows // chunk, body, 0)

    def expert_stage(mb):
        block = min(256, rows)
        peers = block // per_peer

        def body(i, carry):
            at = pl.multiple_of(i * block, block)
            incoming = routed[mb, pl.ds(i * peers, peers)].reshape(block, width)
            grad = lax.dot_general(
                incoming, w2d[...], (((1,), (1,)), ((), ())), preferred_element_type=F32
            )
            out = (grad * factor[mb, pl.ds(at, block), :]).astype(BF16)
            fog[mb, pl.ds(at, block), :] = out
            back = lax.dot_general(
                out, w1v[...], (((1,), (1,)), ((), ())), preferred_element_type=F32
            ).astype(BF16)
            rsend[mb, pl.ds(i * peers, peers)] = back.reshape(peers, per_peer, width)
            return carry

        lax.fori_loop(0, rows // block, body, 0)
        for by in range(1, nyc):
            r_copy(mb, by).start()
        own_return(mb).start()

    def combine(mb):
        for by in range(1, nyc):
            r_arrival(mb, by).wait_recv()
        own_return(mb).wait()

        def partial_sums(pair):
            back = jnp.concatenate(
                [rrecv[mb, yc, pair * 2 * PAD : (pair + 1) * 2 * PAD, :] for yc in range(nyc)],
                axis=0,
            )
            part[pair] = jnp.dot(comb[mb, pair], back, preferred_element_type=F32)

        def partial_of(at, half):
            return part[
                at // 2,
                (at % 2) * tok : (at % 2 + 1) * tok,
                half * half_cols : (half + 1) * half_cols,
            ]

        def send(direction, step, half, value):
            ring_send[
                mb, direction, step - 1, :, half * half_cols : (half + 1) * half_cols
            ] = value.astype(BF16)
            q_copy(mb, direction, step, half).start()

        def received(direction, step, half):
            q_copy(mb, direction, step, half).wait_recv()
            return ring_recv[
                mb, direction, step - 1, :, half * half_cols : (half + 1) * half_cols
            ].astype(F32)

        partial_sums(3)
        send(RIGHT, 1, 0, partial_of(7, 0))
        send(LEFT, 1, 1, partial_of(7, 1))
        partial_sums(2)
        send(RIGHT, 2, 1, partial_of(6, 1))
        send(LEFT, 2, 0, partial_of(5, 0))
        partial_sums(1)
        partial_sums(0)
        send(RIGHT, 2, 0, partial_of(6, 0) + received(RIGHT, 1, 0))
        send(LEFT, 2, 1, partial_of(5, 1) + received(LEFT, 1, 1))
        for step in (3, 4):
            for half in ((1, 0) if step == 3 else (1, 0)):
                for direction in (RIGHT, LEFT):
                    at = block_of(LEFT if direction == RIGHT else RIGHT, 5 - step)
                    send(
                        direction,
                        step,
                        half,
                        partial_of(at, half) + received(direction, step - 1, half),
                    )
        for half in (1, 0):
            cols = slice(half * half_cols, (half + 1) * half_cols)
            total = gath[mb, 0, 0:tok, cols].astype(F32) + partial_of(0, half)
            total = total + received(RIGHT, 4, half) + received(LEFT, 4, half)
            gout[mb, :, cols] = total.astype(BF16)

            @pl.when(pipe > 0)
            def _():
                x_copy(mb, half).start()

        sec_out[mb] = gout[mb]

    def finish_return(mb):
        for by in range(1, nyc):
            r_arrival(mb, by).wait_send()
        for half, direction in streams(4):
            q_copy(mb, direction, 1, half).wait_send()
        for step in range(2, 5):
            for half, direction in streams(1):
                q_copy(mb, direction, step, half).wait_send()

        @pl.when(pipe > 0)
        def _():
            for half in range(2):
                x_copy(mb, half).wait_send()

    def turn_body(turn, carry):
        mb, is_grad, is_any, task = plan(turn)

        @pl.when(is_any)
        def _():
            @pl.when(is_grad & (pipe < sections - 1))
            def _():
                for half in (1, 0):
                    x_copy(mb, half).wait_recv()

            @pl.when(turn > 0)
            def _():
                ring_start(task)

            gather(task)

        @pl.when(turn == 0)
        def _():
            for copy in weight_copies:
                copy.wait()

        @pl.when(turn < 2)
        def _():
            factors(turn)

        @pl.when(is_any)
        def _():
            finish_gather(task)

        @pl.when(is_grad)
        def _():
            expert_stage(mb)
            combine(mb)
            finish_return(mb)

        @pl.when(is_any)
        def _():
            finish_sends(task)

        return carry

    lax.fori_loop(0, sections + 1, turn_body, 0)
    for by in range(1, NZ):
        selection_copy(by).wait_send()

    both_rows = 2 * rows
    tile = 256
    grads = routed[0:2].reshape(both_rows, width)
    for start in range(0, hidden, tile):
        stop = min(start + tile, hidden)
        lanes = act[:, start : min(start + tile, act.shape[1])]
        g2 = lax.dot_general(lanes, grads, (((0,), (0,)), ((), ())), preferred_element_type=F32)
        g2_out[start:stop, :] = g2[: stop - start].astype(BF16)
    outs = fog[...].reshape(both_rows, wide)

    def g1_body(i, carry):
        at = pl.multiple_of(i * tile, tile)
        lanes = routed[2:4, :, :, pl.ds(at, tile)].reshape(both_rows, tile)
        g1 = lax.dot_general(lanes, outs, (((0,), (0,)), ((), ())), preferred_element_type=F32)
        g1_out[pl.ds(at, tile), :] = g1.astype(BF16)
        return carry

    lax.fori_loop(0, width // tile, g1_body, 0)


def selection(ids, gates, experts):
    micro, tok, top = ids.shape
    flat = ids.reshape(micro, tok * top)
    order = jnp.arange(tok * top)
    earlier = (flat[:, :, None] == flat[:, None, :]) & (order[None, :] < order[:, None])[None]
    slot = jnp.sum(earlier.astype(jnp.int32), axis=2)
    target = (flat * PAD + slot).reshape(micro * tok, top)
    row = lax.broadcasted_iota(jnp.int32, (experts * PAD, micro * tok), 0)
    weight = gates.reshape(micro * tok, top)
    out = jnp.zeros((experts * PAD, micro * tok), F32)
    for k in range(top):
        out = out + jnp.where(row == target[None, :, k], weight[None, :, k], 0.0)
    return out.astype(BF16)


def per_device(cotangent, expert_ids, gates, layer_inputs, saved_fc1, w_fc1, w_fc2):
    experts = lax.axis_size("expert")
    sections = lax.axis_size("pipe")
    nyc = experts // NZ
    micro, tok, width = cotangent.shape
    slots, wide = saved_fc1.shape[3:]
    hidden = wide // 2
    cap = slots // experts
    rows = experts * PAD
    per_peer = NZ * PAD
    smat = selection(expert_ids[0], gates[0], experts)
    dims = (sections, nyc, tok, width, wide, cap)
    vmem = pl.BlockSpec(memory_space=pltpu.VMEM)
    hbm = pl.BlockSpec(memory_space=pl.ANY)
    act_width = -(-hidden // 256) * 256
    dma = pltpu.SemaphoreType.DMA
    out = pl.pallas_call(
        functools.partial(fused_kernel, dims),
        out_shape=(
            jax.ShapeDtypeStruct((micro, tok, width), BF16),
            jax.ShapeDtypeStruct((width, wide), BF16),
            jax.ShapeDtypeStruct((hidden, width), BF16),
        ),
        in_specs=[vmem, vmem, vmem, hbm, hbm, hbm],
        out_specs=(vmem, vmem, vmem),
        scratch_shapes=[
            pltpu.VMEM((4, NZ // 2, 2 * tok, width), BF16),
            pltpu.VMEM((4, nyc, per_peer, width), BF16),
            pltpu.VMEM((4, nyc, per_peer, width), BF16),
            pltpu.VMEM((2, nyc, per_peer, width), BF16),
            pltpu.VMEM((2, nyc, per_peer, width), BF16),
            pltpu.VMEM((NZ // 2, 2 * tok, width), F32),
            pltpu.VMEM((2, 2, 4, tok, width), BF16),
            pltpu.VMEM((2, 2, 4, tok, width), BF16),
            pltpu.VMEM((2, tok, width), BF16),
            pltpu.VMEM((NZ, nyc * PAD, 2 * tok), BF16),
            pltpu.VMEM((4, NZ // 2, 2 * nyc * PAD, 2 * tok), BF16),
            pltpu.VMEM((2, NZ // 2, 2 * tok, 2 * nyc * PAD), BF16),
            pltpu.VMEM((width, wide), BF16),
            pltpu.VMEM((wide, width), BF16),
            pltpu.VMEM((2, rows, wide), BF16),
            pltpu.VMEM((2, rows, wide), F32),
            pltpu.VMEM((2 * rows, act_width), BF16),
            pltpu.VMEM((2, rows, wide), BF16),
            dma((4, 2, 4, 2)),
            dma((4, 2, 4, 2)),
            dma((4, nyc)),
            dma((4, nyc)),
            dma((2, nyc)),
            dma((2, nyc)),
            dma((2, 2, 4, 2)),
            dma((2, 2, 4, 2)),
            dma((2, 2)),
            dma((2, 2)),
            dma((NZ,)),
            dma((NZ,)),
            dma((5,)),
            dma((6,)),
        ],
        compiler_params=pltpu.CompilerParams(
            collective_id=0, has_side_effects=True, vmem_limit_bytes=60 * 1024 * 1024
        ),
        name="split_backward",
    )(cotangent, smat, layer_inputs[0], saved_fc1[0, :, 0], w_fc1[0, 0], w_fc2[0, 0])
    return out[0][None], out[1][None, None], out[2][None, None]


def solution(mesh):
    in_specs = (
        P(None, "expert", None),
        P("pipe", None, "expert", None),
        P("pipe", None, "expert", None),
        P("pipe", None, "expert", None),
        P("pipe", None, "expert", None, None),
        P("pipe", "expert", None, None),
        P("pipe", "expert", None, None),
    )
    out_specs = (
        P("pipe", None, "expert", None),
        P("pipe", "expert", None, None),
        P("pipe", "expert", None, None),
    )
    return jax.shard_map(
        per_device, mesh=mesh, in_specs=in_specs, out_specs=out_specs, check_vma=False
    )
```

```python
import functools

import jax
import jax.numpy as jnp
from jax import lax
from jax.experimental import pallas as pl
from jax.experimental.pallas import tpu as pltpu
from jax.sharding import PartitionSpec as P

MESH = pl.DeviceIdType.MESH
NZ = 8
PAD = 8
F32, BF16 = jnp.float32, jnp.bfloat16


SUMS = {
    0: (1, (0, 1), 6),
    1: (2, (0,), 7),
    2: (-1, (0, 1), 5),
    3: (-2, (1,), 7),
    4: (2, (0, 1), 4),
    5: (-2, (0, 1), 3),
    6: (1, (0, 1), 2),
    7: (-1, (0, 1), 1),
}


def fused_kernel(
    dims,
    cot,
    smat,
    xin,
    saved_hbm,
    w1_hbm,
    w2_hbm,
    sec_out,
    g1_out,
    g2_out,
    gath,
    sendb,
    routed,
    rsend,
    rrecv,
    part,
    sum_send,
    sum_recv,
    gout,
    srecv,
    sel,
    comb,
    w1v,
    w2d,
    savedv,
    factor,
    act,
    fog,
    d_send,
    e_send,
    f_send,
    z_recv,
    y_send,
    y_recv,
    r_send,
    r_recv,
    q_send,
    q_recv,
    s_send,
    s_recv,
    local_sem,
):
    sections, nyc, tok, width, wide, cap = dims
    hidden = wide // 2
    half_cols = width // 2
    rows_in = NZ * nyc * cap
    rows = NZ * nyc * PAD
    per_peer = NZ * PAD
    pair_rows = 2 * nyc * PAD
    sel_rows = nyc * PAD
    group = nyc // 2

    pipe = lax.axis_index("pipe")
    expert = lax.axis_index("expert")
    zi = expert // nyc
    me = expert % nyc
    core = me % 2
    place = core * group + me // 2

    def along_z(by, plane=None):
        return (pipe if plane is None else plane, ((zi + by + NZ) % NZ) * nyc + me)

    def along_y(yc):
        return (pipe, zi * nyc + yc)

    is_last = pipe == sections - 1
    before = (pipe + sections - 1) % sections
    after = (pipe + 1) % sections

    weight_copies = (
        pltpu.make_async_copy(w1_hbm, w1v, local_sem.at[0]),
        pltpu.make_async_copy(w2_hbm, w2d.at[pl.ds(0, hidden), :], local_sem.at[1]),
        pltpu.make_async_copy(w2_hbm, w2d.at[pl.ds(hidden, hidden), :], local_sem.at[2]),
        pltpu.make_async_copy(saved_hbm.at[0], savedv.at[0, pl.ds(0, rows_in), :], local_sem.at[3]),
        pltpu.make_async_copy(saved_hbm.at[1], savedv.at[1, pl.ds(0, rows_in), :], local_sem.at[4]),
    )

    barrier = pltpu.get_barrier_semaphore()
    for by in range(1, NZ):
        pl.semaphore_signal(barrier, inc=1, device_id=along_z(by), device_id_type=MESH)
    for by in range(1, nyc):
        pl.semaphore_signal(
            barrier, inc=1, device_id=along_y((me + by) % nyc), device_id_type=MESH
        )
    for by in range(-2, 3):
        for plane in (before, after):
            pl.semaphore_signal(
                barrier, inc=1, device_id=along_z(by, plane), device_id_type=MESH
            )

    for copy in weight_copies:
        copy.start()
    for mb in range(2):
        gath[2 + mb, 0, 0:tok, :] = xin[mb]
        if rows > rows_in:
            savedv[mb, rows_in:rows, :] = jnp.zeros((rows - rows_in, wide), BF16)

    @pl.when(is_last)
    def _():
        for mb in range(2):
            gath[mb, 0, 0:tok, :] = cot[mb]

    srecv[0] = smat[pl.ds(pl.multiple_of(zi * sel_rows, sel_rows), sel_rows), :]
    pl.semaphore_wait(barrier, NZ + nyc - 2 + 10)

    def selection_copy(by):
        at = 2 * by - 1 if by <= 4 else 2 * (NZ - by)
        to = (zi + by) % NZ
        return pltpu.make_async_remote_copy(
            src_ref=smat.at[pl.ds(pl.multiple_of(to * sel_rows, sel_rows), sel_rows), :],
            dst_ref=srecv.at[at],
            send_sem=s_send.at[by],
            recv_sem=s_recv.at[at],
            device_id=along_z(by),
            device_id_type=MESH,
        )

    def block_view(task, at, half):
        return gath.at[
            task, at // 2, pl.ds((at % 2) * tok, tok), pl.ds(half * half_cols, half_cols)
        ]

    def spread_copy(src, task, by, at, half, sem, plane=None):
        return pltpu.make_async_remote_copy(
            src_ref=src,
            dst_ref=block_view(task, at, half),
            send_sem=sem,
            recv_sem=z_recv.at[task, at, half],
            device_id=along_z(by, plane),
            device_id_type=MESH,
        )

    def spread_own(task):
        for by, at in ((2, 3), (-2, 4), (1, 1), (-1, 2)):
            for half in range(2):
                src = block_view(task, 0, half)
                spread_copy(src, task, by, at, half, d_send.at[task]).start()

    def spread_on(mb):
        for by, at in ((2, 3), (-2, 4), (1, 1), (-1, 2), (0, 0)):
            for half in range(2):
                src = gout.at[mb, :, pl.ds(half * half_cols, half_cols)]
                spread_copy(src, mb, by, at, half, e_send.at[mb], before).start()

    def wait_block(task, at, half):
        wait_for(block_view(task, at, half), z_recv.at[task, at, half])

    def y_copy(task, by, at, count):
        to = (me + by) % nyc
        return pltpu.make_async_remote_copy(
            src_ref=sendb.at[task, to, pl.ds(at, count), :],
            dst_ref=routed.at[task, place, pl.ds(at, count), :],
            send_sem=y_send.at[task],
            recv_sem=y_recv.at[task, core],
            device_id=along_y(to),
            device_id_type=MESH,
        )

    def own_copy(task):
        return pltpu.make_async_copy(
            sendb.at[task, me], routed.at[task, place], y_recv.at[task, core]
        )

    def wait_for(ref, sem):
        pltpu.make_async_copy(ref, ref, sem).wait()

    def wait_rows(task, of_core):
        wait_for(
            routed.at[task, pl.ds(of_core * group, group)], y_recv.at[task, of_core]
        )

    def r_copy(mb, pair, to):
        at = (to % 2) * group + to // 2
        return pltpu.make_async_remote_copy(
            src_ref=rsend.at[mb, at, pl.ds(pair * 2 * PAD, 2 * PAD), :],
            dst_ref=rrecv.at[mb, pair, me],
            send_sem=r_send.at[mb, to % 2],
            recv_sem=r_recv.at[mb, pair],
            device_id=along_y(to),
            device_id_type=MESH,
        )

    def own_return(mb, pair):
        return pltpu.make_async_copy(
            rsend.at[mb, place, pl.ds(pair * 2 * PAD, 2 * PAD), :],
            rrecv.at[mb, pair, me],
            r_recv.at[mb, pair],
        )

    def q_copy(mb, slot, half):
        cols = pl.ds(half * half_cols, half_cols)
        return pltpu.make_async_remote_copy(
            src_ref=sum_send.at[mb, slot, :, cols],
            dst_ref=sum_recv.at[mb, slot, :, cols],
            send_sem=q_send.at[mb],
            recv_sem=q_recv.at[mb, slot],
            device_id=along_z(SUMS[slot][0]),
            device_id_type=MESH,
        )

    def plan(turn):
        chunk_no = turn - 2
        is_chunk = (turn >= 2) & (turn < 6)
        mb, of_core = (turn - 2) // 2, turn % 2
        is_own = is_chunk & (of_core == core)
        is_x = ((turn < 2) & jnp.logical_not(is_last)) | ((turn >= 6) & is_last)
        task = jnp.where(is_chunk, mb, 2 + turn % 2)
        is_done = (turn >= 3) & (turn <= 6) & (of_core != core)
        is_done = is_done & jnp.logical_not((turn == 6) & (pipe == 0))
        return mb, of_core, is_chunk, is_own, is_own | is_x, task, is_done, (chunk_no - 1) // 2

    @pl.when(is_last & (core == 0))
    def _():
        spread_own(0)

    for by in range(1, NZ):
        selection_copy(by).start()

    @pl.when(jnp.logical_not(is_last))
    def _():
        spread_own(2)
        spread_own(3)

    lane = lax.broadcasted_iota(jnp.int32, (sel_rows, 2 * tok), 1)
    low = lane < tok
    for by in range(1, NZ):
        selection_copy(by).wait_recv()
    for pair in range(NZ // 2):
        first, second = srecv[2 * pair].astype(F32), srecv[2 * pair + 1].astype(F32)
        for mb in range(2):
            one = first if mb == 0 else pltpu.roll(first, tok, 1)
            two = second if mb == 1 else pltpu.roll(second, tok, 1)
            one = jnp.where(low, one, 0.0)
            two = jnp.where(low, 0.0, two)
            pieces = []
            for yc in range(nyc):
                pieces += [one[yc * PAD : (yc + 1) * PAD], two[yc * PAD : (yc + 1) * PAD]]
            both = jnp.concatenate(pieces, axis=0)
            ones = jnp.where(both != 0.0, 1.0, 0.0)
            sel[mb, pair] = both.astype(BF16)
            sel[2 + mb, pair] = ones.astype(BF16)
            comb[mb, pair] = ones.T.astype(BF16)

    @pl.when(is_last & (core == 1))
    def _():
        spread_own(0)

    def select(task, pair):
        chosen = jnp.dot(sel[task, pair], gath[task, pair], preferred_element_type=F32).astype(BF16)
        at = pair * 2 * PAD
        for yc in range(nyc):
            sendb[task, yc, at : at + 2 * PAD, :] = chosen[yc * 2 * PAD : (yc + 1) * 2 * PAD]
        for by in range(1, nyc):
            y_copy(task, by, at, 2 * PAD).start()

    def gather(task, is_handed_on):
        def forward(from_at, by, at, half):
            src = block_view(task, from_at, half)
            spread_copy(src, task, by, at, half, f_send.at[task]).start()

        wait_block(task, 3, 0)
        forward(3, 2, 7, 0)
        forward(3, 1, 5, 0)
        wait_block(task, 4, 1)
        forward(4, -2, 7, 1)
        forward(4, -1, 6, 1)
        wait_block(task, 3, 1)
        forward(3, 1, 5, 1)
        wait_block(task, 4, 0)
        forward(4, -1, 6, 0)
        for half in range(2):
            wait_block(task, 1, half)

        @pl.when(is_handed_on)
        def _():
            for half in range(2):
                wait_block(task, 0, half)

        select(task, 0)
        for pair, needs in ((1, (2,)), (2, (5,)), (3, (6, 7))):
            for at in needs:
                for half in range(2):
                    wait_block(task, at, half)
            select(task, pair)
        own_copy(task).start()

    chunk = min(128, rows)

    half_rows = rows // 2

    def factors(mb, of_core):
        def body(i, carry):
            at = pl.multiple_of(of_core * half_rows + i * chunk, chunk)
            row = lax.broadcasted_iota(jnp.int32, (chunk, rows), 0) + at
            col = lax.broadcasted_iota(jnp.int32, (chunk, rows), 1)
            peer = row // per_peer
            yc = (peer % group) * 2 + peer // group
            block = (row // PAD) % NZ
            slot = row % PAD
            rel = jnp.where(block % 2 == 1, NZ - (block + 1) // 2, block // 2)
            zz = (zi + rel) % NZ
            want = zz * (nyc * cap) + yc * cap + slot
            pick = jnp.where((col == want) & (slot < cap), 1.0, 0.0).astype(BF16)
            val = jnp.dot(pick, savedv[mb], preferred_element_type=F32)
            swapped = pltpu.roll(val, hidden, 1)
            is_gate = lax.broadcasted_iota(jnp.int32, (chunk, wide), 1) < hidden
            a = jnp.where(is_gate, val, swapped)
            u = jnp.where(is_gate, swapped, val)
            sg = jax.nn.sigmoid(a)
            silu = a * sg
            factor[mb, pl.ds(at, chunk), :] = jnp.where(
                is_gate, u * (sg * (1.0 + a * (1.0 - sg))), silu
            )
            act[pl.ds(mb * rows + at, chunk), :] = (silu * u)[:, : act.shape[1]].astype(BF16)
            return carry

        lax.fori_loop(0, half_rows // chunk, body, 0)

    def expert_stage(mb, of_core):
        at = pl.multiple_of(of_core * half_rows, half_rows)
        peers = pl.ds(of_core * group, group)
        incoming = routed[mb, peers].reshape(half_rows, width)
        grad = lax.dot_general(
            incoming, w2d[...], (((1,), (1,)), ((), ())), preferred_element_type=F32
        )
        out = (grad * factor[mb, pl.ds(at, half_rows), :]).astype(BF16)
        fog[mb, pl.ds(at, half_rows), :] = out
        back = lax.dot_general(
            out, w1v[...], (((1,), (1,)), ((), ())), preferred_element_type=F32
        ).astype(BF16)
        rsend[mb, peers] = back.reshape(group, per_peer, width)
        for pair in (3, 2, 1, 0):
            for by in range(group):
                to = ((me // 2 + by) % group) * 2 + of_core
                if by > 0:
                    r_copy(mb, pair, to).start()
                else:

                    @pl.when(of_core == core)
                    def _():
                        own_return(mb, pair).start()

                    @pl.when(of_core != core)
                    def _():
                        r_copy(mb, pair, to).start()

    def half_of(half):
        return slice(half * half_cols, (half + 1) * half_cols)

    def partial_of(at, half):
        return part[at // 2, (at % 2) * tok : (at % 2 + 1) * tok, half_of(half)]

    def combine(mb):
        def partial_sums(pair):
            wait_for(rrecv.at[mb, pair], r_recv.at[mb, pair])
            back = rrecv[mb, pair].reshape(pair_rows, width)
            part[pair] = jnp.dot(comb[mb, pair], back, preferred_element_type=F32)

        def send(slot, extra=None):
            for half in SUMS[slot][1]:
                value = partial_of(SUMS[slot][2], half)
                if extra is not None:
                    value = value + sum_recv[mb, extra[0], :, half_of(half)].astype(F32)
                    if half in SUMS[extra[1]][1]:
                        value = value + sum_recv[mb, extra[1], :, half_of(half)].astype(F32)
                sum_send[mb, slot, :, half_of(half)] = value.astype(BF16)
                q_copy(mb, slot, half).start()

        def wait_sum(slot):
            if len(SUMS[slot][1]) == 2:
                wait_for(sum_recv.at[mb, slot], q_recv.at[mb, slot])
            else:
                half = SUMS[slot][1][0]
                cols = pl.ds(half * half_cols, half_cols)
                wait_for(sum_recv.at[mb, slot, :, cols], q_recv.at[mb, slot])

        partial_sums(3)
        send(1)
        send(3)
        send(0)
        partial_sums(2)
        send(2)
        partial_sums(1)
        partial_sums(0)
        wait_sum(0)
        wait_sum(1)
        send(4, (0, 1))
        wait_sum(2)
        wait_sum(3)
        send(5, (2, 3))
        send(6)
        send(7)

    def finish(mb):
        for slot in (6, 7, 4, 5):
            wait_for(sum_recv.at[mb, slot], q_recv.at[mb, slot])
        for half in range(2):
            cols = half_of(half)
            total = gath[mb, 0, 0:tok, cols].astype(F32) + partial_of(0, half)
            for slot in (6, 7, 4, 5):
                total = total + sum_recv[mb, slot, :, cols].astype(F32)
            gout[mb, :, cols] = total.astype(BF16)

        @pl.when(pipe > 0)
        def _():
            spread_on(mb)

        sec_out[mb] = gout[mb]

    def turn_body(turn, carry):
        mb, of_core, is_chunk, is_own, is_gather, task, is_done, done_mb = plan(turn)

        @pl.when(is_gather)
        def _():
            gather(task, is_own & jnp.logical_not(is_last))

        @pl.when(turn == 0)
        def _():
            for copy in weight_copies:
                copy.wait()

            @pl.when(jnp.logical_not(is_last))
            def _():
                def body(some, carry):
                    factors(some // 2, some % 2)
                    return carry

                lax.fori_loop(0, 4, body, 0)

        @pl.when(is_chunk)
        def _():
            @pl.when(is_last)
            def _():
                factors(mb, of_core)

            wait_rows(mb, of_core)
            expert_stage(mb, of_core)

        @pl.when(is_own)
        def _():
            combine(mb)

            @pl.when(is_last)
            def _():
                @pl.when(mb == 0)
                def _():
                    spread_own(1)

                @pl.when(mb == 1)
                def _():
                    spread_own(2)
                    spread_own(3)

        @pl.when(is_done)
        def _():
            finish(done_mb)

        return carry

    lax.fori_loop(0, 8, turn_body, 0)
    for task in (2, 3):
        for of_core in range(2):
            wait_rows(task, of_core)
    both_rows = 2 * rows
    tile = 256
    grads = routed[0:2].reshape(both_rows, width)
    for start in range(0, hidden, tile):
        stop = min(start + tile, hidden)
        lanes = act[:, start : min(start + tile, act.shape[1])]
        g2 = lax.dot_general(lanes, grads, (((0,), (0,)), ((), ())), preferred_element_type=F32)
        g2_out[start:stop, :] = g2[: stop - start].astype(BF16)
    outs = fog[...].reshape(both_rows, wide)

    def g1_body(i, carry):
        at = pl.multiple_of(i * tile, tile)
        lanes = routed[2:4, :, :, pl.ds(at, tile)].reshape(both_rows, tile)
        g1 = lax.dot_general(lanes, outs, (((0,), (0,)), ((), ())), preferred_element_type=F32)
        g1_out[pl.ds(at, tile), :] = g1.astype(BF16)
        return carry

    lax.fori_loop(0, width // tile, g1_body, 0)

    @pl.when((pipe == 0) & (core == 1))
    def _():
        finish(1)

    for by in range(1, NZ):
        selection_copy(by).wait_send()
    for task in range(4):
        for sem, blocks in ((f_send, 3), (y_send, nyc - 1)):
            wait_for(sendb.at[task, pl.ds(0, blocks)], sem.at[task])
        if task >= 2:
            wait_for(sendb.at[task, pl.ds(0, 4)], d_send.at[task])

    @pl.when(is_last)
    def _():
        for mb in range(2):
            wait_for(sendb.at[mb, pl.ds(0, 4)], d_send.at[mb])

    @pl.when(pipe > 0)
    def _():
        for mb in range(2):
            wait_for(sendb.at[mb, pl.ds(0, 5)], e_send.at[mb])

    for mb in range(2):
        wait_for(sendb.at[mb, pl.ds(0, 7)], q_send.at[mb])
        wait_for(rsend.at[mb, pl.ds(0, group - 1)], r_send.at[mb, core])
        wait_for(rsend.at[mb, pl.ds(0, group)], r_send.at[mb, 1 - core])


def selection(ids, gates, experts):
    micro, tok, top = ids.shape
    flat = ids.reshape(micro, tok * top)
    order = jnp.arange(tok * top)
    earlier = (flat[:, :, None] == flat[:, None, :]) & (order[None, :] < order[:, None])[None]
    slot = jnp.sum(earlier.astype(jnp.int32), axis=2)
    target = (flat * PAD + slot).reshape(micro * tok, top)
    row = lax.broadcasted_iota(jnp.int32, (experts * PAD, micro * tok), 0)
    weight = gates.reshape(micro * tok, top)
    out = jnp.zeros((experts * PAD, micro * tok), F32)
    for k in range(top):
        out = out + jnp.where(row == target[None, :, k], weight[None, :, k], 0.0)
    return out.astype(BF16)


def per_device(cotangent, expert_ids, gates, layer_inputs, saved_fc1, w_fc1, w_fc2):
    experts = lax.axis_size("expert")
    sections = lax.axis_size("pipe")
    nyc = experts // NZ
    micro, tok, width = cotangent.shape
    slots, wide = saved_fc1.shape[3:]
    hidden = wide // 2
    cap = slots // experts
    rows = experts * PAD
    per_peer = NZ * PAD
    smat = selection(expert_ids[0], gates[0], experts)
    dims = (sections, nyc, tok, width, wide, cap)
    vmem = pl.BlockSpec(memory_space=pltpu.VMEM)
    hbm = pl.BlockSpec(memory_space=pl.ANY)
    act_width = -(-hidden // 256) * 256
    dma = pltpu.SemaphoreType.DMA
    out = pl.pallas_call(
        functools.partial(fused_kernel, dims),
        out_shape=(
            jax.ShapeDtypeStruct((micro, tok, width), BF16),
            jax.ShapeDtypeStruct((width, wide), BF16),
            jax.ShapeDtypeStruct((hidden, width), BF16),
        ),
        in_specs=[vmem, vmem, vmem, hbm, hbm, hbm],
        out_specs=(vmem, vmem, vmem),
        scratch_shapes=[
            pltpu.VMEM((4, NZ // 2, 2 * tok, width), BF16),
            pltpu.VMEM((4, nyc, per_peer, width), BF16),
            pltpu.VMEM((4, nyc, per_peer, width), BF16),
            pltpu.VMEM((2, nyc, per_peer, width), BF16),
            pltpu.VMEM((2, NZ // 2, nyc, 2 * PAD, width), BF16),
            pltpu.VMEM((NZ // 2, 2 * tok, width), F32),
            pltpu.VMEM((2, 8, tok, width), BF16),
            pltpu.VMEM((2, 8, tok, width), BF16),
            pltpu.VMEM((2, tok, width), BF16),
            pltpu.VMEM((NZ, nyc * PAD, 2 * tok), BF16),
            pltpu.VMEM((4, NZ // 2, 2 * nyc * PAD, 2 * tok), BF16),
            pltpu.VMEM((2, NZ // 2, 2 * tok, 2 * nyc * PAD), BF16),
            pltpu.VMEM((width, wide), BF16),
            pltpu.VMEM((wide, width), BF16),
            pltpu.VMEM((2, rows, wide), BF16),
            pltpu.VMEM((2, rows, wide), F32),
            pltpu.VMEM((2 * rows, act_width), BF16),
            pltpu.VMEM((2, rows, wide), BF16),
            dma((4,)),
            dma((2,)),
            dma((4,)),
            dma((4, 8, 2)),
            dma((4,)),
            dma((4, 2)),
            dma((2, 2)),
            dma((2, 4)),
            dma((2,)),
            dma((2, 8)),
            dma((NZ,)),
            dma((NZ,)),
            dma((5,)),
        ],
        compiler_params=pltpu.CompilerParams(
            collective_id=0, has_side_effects=True, vmem_limit_bytes=60 * 1024 * 1024
        ),
        name="split_backward",
    )(cotangent, smat, layer_inputs[0], saved_fc1[0, :, 0], w_fc1[0, 0], w_fc2[0, 0])
    return out[0][None], out[1][None, None], out[2][None, None]


def solution(mesh):
    in_specs = (
        P(None, "expert", None),
        P("pipe", None, "expert", None),
        P("pipe", None, "expert", None),
        P("pipe", None, "expert", None),
        P("pipe", None, "expert", None, None),
        P("pipe", "expert", None, None),
        P("pipe", "expert", None, None),
    )
    out_specs = (
        P("pipe", None, "expert", None),
        P("pipe", "expert", None, None),
        P("pipe", "expert", None, None),
    )
    return jax.shard_map(
        per_device, mesh=mesh, in_specs=in_specs, out_specs=out_specs, check_vma=False
    )
```

```python
import functools

import jax
import jax.numpy as jnp
from jax import lax
from jax.experimental import pallas as pl
from jax.experimental.pallas import tpu as pltpu
from jax.sharding import PartitionSpec as P

MESH = pl.DeviceIdType.MESH
NZ = 8
PAD = 8
F32, BF16 = jnp.float32, jnp.bfloat16


SUMS = {
    0: (1, (0, 1), 6),
    1: (2, (0,), 7),
    2: (-1, (0, 1), 5),
    3: (-2, (1,), 7),
    4: (2, (0, 1), 4),
    5: (-2, (0, 1), 3),
    6: (1, (0, 1), 2),
    7: (-1, (0, 1), 1),
}


def fused_kernel(
    dims,
    cot,
    ids,
    gates,
    xin,
    saved_hbm,
    w1_hbm,
    w2_hbm,
    sec_out,
    g1_out,
    g2_out,
    gath,
    sendb,
    routed,
    rsend,
    rrecv,
    part,
    sum_send,
    sum_recv,
    gout,
    stage,
    smat,
    srecv,
    sel,
    comb,
    w1v,
    w2d,
    savedv,
    factor,
    act,
    fog,
    d_send,
    e_send,
    f_send,
    z_recv,
    y_send,
    y_recv,
    r_send,
    r_recv,
    q_send,
    q_recv,
    s_send,
    s_recv,
    o_send,
    o_recv,
    h_send,
    local_sem,
):
    sections, nyc, tok, width, wide, cap = dims
    hidden = wide // 2
    side = width // 2
    half_cols = side // 2
    rows_in = NZ * nyc * cap
    rows = NZ * nyc * PAD
    per_peer = NZ * PAD
    pair_rows = 2 * nyc * PAD
    sel_rows = nyc * PAD
    group = nyc // 2

    pipe = lax.axis_index("pipe")
    expert = lax.axis_index("expert")
    zi = expert // nyc
    me = expert % nyc
    core = me % 2

    other = 1 - core
    sibling = me + 1 - 2 * core

    def along_z(by, plane=None, to=None):
        at = ((zi + by + NZ) % NZ) * nyc + (me if to is None else to)
        return (pipe if plane is None else plane, at)

    def along_y(yc):
        return (pipe, zi * nyc + yc)

    is_last = pipe == sections - 1
    before = (pipe + sections - 1) % sections
    after = (pipe + 1) % sections

    weight_copies = (
        pltpu.make_async_copy(w1_hbm, w1v, local_sem.at[0]),
        pltpu.make_async_copy(w2_hbm, w2d.at[pl.ds(0, hidden), :], local_sem.at[1]),
        pltpu.make_async_copy(w2_hbm, w2d.at[pl.ds(hidden, hidden), :], local_sem.at[2]),
        pltpu.make_async_copy(saved_hbm.at[0], savedv.at[0, pl.ds(0, rows_in), :], local_sem.at[3]),
        pltpu.make_async_copy(saved_hbm.at[1], savedv.at[1, pl.ds(0, rows_in), :], local_sem.at[4]),
    )

    barrier = pltpu.get_barrier_semaphore()
    for by in range(1, NZ):
        pl.semaphore_signal(barrier, inc=1, device_id=along_z(by), device_id_type=MESH)
        pl.semaphore_signal(
            barrier, inc=1, device_id=along_z(by, to=sibling), device_id_type=MESH
        )
    for by in range(1, nyc):
        pl.semaphore_signal(
            barrier, inc=1, device_id=along_y((me + by) % nyc), device_id_type=MESH
        )
    for by in range(-2, 3):
        for plane in (before, after):
            pl.semaphore_signal(
                barrier, inc=1, device_id=along_z(by, plane), device_id_type=MESH
            )

    for copy in weight_copies:
        copy.start()
    for mb in range(2):
        if rows > rows_in:
            savedv[mb, rows_in:rows, :] = jnp.zeros((rows - rows_in, wide), BF16)

    experts = NZ * nyc
    lanes_two = 2 * tok
    named = lax.broadcasted_iota(jnp.int32, (experts, lanes_two), 0)
    hit = jnp.zeros((experts, lanes_two), F32)
    weight = jnp.zeros((experts, lanes_two), F32)
    for k in range(ids.shape[0]):
        of_k = jnp.concatenate([ids[k, 0:1, :], ids[k, 1:2, :]], axis=1)
        gate_k = jnp.concatenate([gates[k, 0:1, :], gates[k, 1:2, :]], axis=1)
        same = named == of_k
        hit = hit + jnp.where(same, 1.0, 0.0)
        weight = weight + jnp.where(same, gate_k, 0.0)
    first = lax.broadcasted_iota(jnp.int32, (lanes_two, lanes_two), 0)
    second = lax.broadcasted_iota(jnp.int32, (lanes_two, lanes_two), 1)
    earlier = (first < second) & ((first < tok) == (second < tok))
    rank = jnp.dot(
        hit.astype(BF16),
        jnp.where(earlier, 1.0, 0.0).astype(BF16),
        preferred_element_type=F32,
    ).astype(jnp.int32)
    slot_no = lax.broadcasted_iota(jnp.int32, (experts, PAD, lanes_two), 1)
    spread_out = jnp.where(rank[:, None, :] == slot_no, weight[:, None, :], 0.0)
    smat[...] = spread_out.reshape(experts * PAD, lanes_two).astype(BF16)

    my_cols = pl.ds(pl.multiple_of(core * side, side), side)
    for mb in range(2):
        gath[2 + mb, core, 0, 0:tok, :] = xin[mb, :, my_cols]

    @pl.when(is_last)
    def _():
        for mb in range(2):
            gath[mb, core, 0, 0:tok, :] = cot[mb, :, my_cols]

    pltpu.make_async_copy(
        smat.at[pl.ds(pl.multiple_of(zi * sel_rows, sel_rows), sel_rows), :],
        srecv.at[core, 0],
        s_recv,
    ).start()
    pl.semaphore_wait(barrier, 2 * (NZ - 1) + nyc - 1 + 10)

    def wait_for(ref, sem):
        pltpu.make_async_copy(ref, ref, sem).wait()

    def selection_copy(by, swap):
        at = 0 if by == 0 else 2 * by - 1 if by <= 4 else 2 * (NZ - by)
        to = (zi + by) % NZ
        return pltpu.make_async_remote_copy(
            src_ref=smat.at[pl.ds(pl.multiple_of(to * sel_rows, sel_rows), sel_rows), :],
            dst_ref=srecv.at[core, at],
            send_sem=s_send.at[1 if swap else 0],
            recv_sem=s_recv,
            device_id=along_z(by, to=sibling if swap else me),
            device_id_type=MESH,
        )

    def block_view(task, of, at, half):
        return gath.at[
            task,
            of,
            at // 2,
            pl.ds((at % 2) * tok, tok),
            pl.ds(half * half_cols, half_cols),
        ]

    def spread_copy(src, task, of, by, at, half, sem, plane=None):
        return pltpu.make_async_remote_copy(
            src_ref=src,
            dst_ref=block_view(task, of, at, half),
            send_sem=sem,
            recv_sem=z_recv.at[task, of, at, half],
            device_id=along_z(by, plane),
            device_id_type=MESH,
        )

    def wait_block(task, of, at, half):
        wait_for(block_view(task, of, at, half), z_recv.at[task, of, at, half])

    def hand_over(source, mb, task):
        for half in range(2):
            at = pl.multiple_of(other * side + half * half_cols, half_cols)
            pltpu.make_async_remote_copy(
                src_ref=source.at[mb, :, pl.ds(at, half_cols)],
                dst_ref=block_view(task, core, 0, half),
                send_sem=h_send.at[task],
                recv_sem=z_recv.at[task, core, 0, half],
                device_id=along_y(sibling),
                device_id_type=MESH,
            ).start()

    def spread_own(task, of):
        @pl.when(other == of)
        def _():
            for half in range(2):
                wait_block(task, of, 0, half)

        for by, at in ((2, 3), (-2, 4), (1, 1), (-1, 2)):
            for half in range(2):
                src = block_view(task, of, 0, half)
                spread_copy(src, task, of, by, at, half, d_send.at[task, of]).start()

    def spread_on(mb, of):
        for by, at in ((2, 3), (-2, 4), (1, 1), (-1, 2), (0, 0)):
            for half in range(2):
                src = gout.at[mb, of, :, pl.ds(half * half_cols, half_cols)]
                spread_copy(src, mb, of, by, at, half, e_send.at[mb, of], before).start()

    def y_copy(task, of, by, at, count):
        to = (me + by) % nyc
        return pltpu.make_async_remote_copy(
            src_ref=sendb.at[task, of, to, pl.ds(at, count), :],
            dst_ref=routed.at[task, core, of * group + me // 2, pl.ds(at, count), :],
            send_sem=y_send.at[task, of],
            recv_sem=y_recv.at[task, of],
            device_id=along_y(to),
            device_id_type=MESH,
        )

    def own_copy(task, of):
        return pltpu.make_async_copy(
            sendb.at[task, of, me],
            routed.at[task, core, of * group + me // 2],
            y_recv.at[task, of],
        )

    def wait_rows(task, of):
        here = routed.at[task, :, pl.ds(of * group, group)]
        wait_for(here, y_recv.at[task, of])

    def r_copy(mb, of, pair, to):
        return pltpu.make_async_remote_copy(
            src_ref=rsend.at[mb, to % 2, of * group + to // 2, pl.ds(pair * 2 * PAD, 2 * PAD), :],
            dst_ref=rrecv.at[mb, of, pair, me],
            send_sem=r_send.at[mb, of],
            recv_sem=r_recv.at[mb, of, pair],
            device_id=along_y(to),
            device_id_type=MESH,
        )

    def own_return(mb, of, pair):
        return pltpu.make_async_copy(
            rsend.at[mb, core, of * group + me // 2, pl.ds(pair * 2 * PAD, 2 * PAD), :],
            rrecv.at[mb, of, pair, me],
            r_recv.at[mb, of, pair],
        )

    def q_copy(mb, of, slot, half):
        cols = pl.ds(half * half_cols, half_cols)
        return pltpu.make_async_remote_copy(
            src_ref=sum_send.at[mb, of, slot, :, cols],
            dst_ref=sum_recv.at[mb, of, slot, :, cols],
            send_sem=q_send.at[mb, of],
            recv_sem=q_recv.at[mb, of, slot],
            device_id=along_z(SUMS[slot][0]),
            device_id_type=MESH,
        )

    def plan(turn):
        chunk_no = turn - 4
        is_chunk = (turn >= 4) & (turn < 8)
        of = turn % 2
        mb = jnp.where(is_chunk, chunk_no // 2, 0)
        is_x = ((turn < 4) & jnp.logical_not(is_last)) | ((turn >= 10) & is_last)
        x_no = jnp.where(turn < 4, turn, turn - 10)
        task = jnp.where(is_chunk, mb, 2 + x_no // 2)
        gather_of = jnp.where(is_chunk, of, x_no % 2)
        is_back = (turn >= 5) & (turn <= 8)
        back_mb = jnp.where(is_back, (turn - 5) // 2, 0)
        is_end = (turn >= 6) & (turn <= 9)
        end_mb = jnp.where(is_end, (turn - 6) // 2, 0)
        back = (is_back, back_mb, (turn + 1) % 2)
        return mb, of, is_chunk, is_chunk | is_x, task, gather_of, back, (is_end, end_mb, of)

    @pl.when(is_last)
    def _():
        hand_over(cot, 0, 0)
        spread_own(0, 0)
        hand_over(cot, 1, 1)

    hand_over(xin, 0, 2)
    hand_over(xin, 1, 3)
    for by in range(NZ):
        for swap in (True, False):
            if by > 0 or swap:
                selection_copy(by, swap).start()

    @pl.when(jnp.logical_not(is_last))
    def _():
        for no in range(4):
            spread_own(2 + no // 2, no % 2)

    lane = lax.broadcasted_iota(jnp.int32, (sel_rows, 2 * tok), 1)
    low = lane < tok
    wait_for(srecv, s_recv)

    def build(of, carry):
        for pair in range(NZ // 2):
            first, second = srecv[of, 2 * pair].astype(F32), srecv[of, 2 * pair + 1].astype(F32)
            for mb in range(2):
                one = first if mb == 0 else pltpu.roll(first, tok, 1)
                two = second if mb == 1 else pltpu.roll(second, tok, 1)
                one = jnp.where(low, one, 0.0)
                two = jnp.where(low, 0.0, two)
                pieces = []
                for yc in range(nyc):
                    pieces += [one[yc * PAD : (yc + 1) * PAD], two[yc * PAD : (yc + 1) * PAD]]
                both = jnp.concatenate(pieces, axis=0)
                ones = jnp.where(both != 0.0, 1.0, 0.0)
                sel[mb, of, pair] = both.astype(BF16)
                sel[2 + mb, of, pair] = ones.astype(BF16)
                comb[mb, of, pair] = ones.T.astype(BF16)
        return carry

    lax.fori_loop(0, 2, build, 0)

    @pl.when(is_last)
    def _():
        spread_own(0, 1)

    def select(task, of, pair):
        chosen = jnp.dot(
            sel[task, of, pair], gath[task, of, pair], preferred_element_type=F32
        ).astype(BF16)
        at = pair * 2 * PAD
        for yc in range(nyc):
            sendb[task, of, yc, at : at + 2 * PAD, :] = chosen[yc * 2 * PAD : (yc + 1) * 2 * PAD]
        for by in range(1, nyc):
            y_copy(task, of, by, at, 2 * PAD).start()

    def gather(task, of, is_handed_on):
        def forward(from_at, by, at, half):
            src = block_view(task, of, from_at, half)
            spread_copy(src, task, of, by, at, half, f_send.at[task, of]).start()

        wait_block(task, of, 3, 0)
        forward(3, 2, 7, 0)
        forward(3, 1, 5, 0)
        wait_block(task, of, 4, 1)
        forward(4, -2, 7, 1)
        forward(4, -1, 6, 1)
        wait_block(task, of, 3, 1)
        forward(3, 1, 5, 1)
        wait_block(task, of, 4, 0)
        forward(4, -1, 6, 0)
        for half in range(2):
            wait_block(task, of, 1, half)

        @pl.when(is_handed_on)
        def _():
            for half in range(2):
                wait_block(task, of, 0, half)

        select(task, of, 0)
        for half in range(2):
            wait_block(task, of, 2, half)
        select(task, of, 1)

    def gather_rest(task, of):
        for pair, needs in ((2, (5,)), (3, (6, 7))):
            for at in needs:
                for half in range(2):
                    wait_block(task, of, at, half)
            select(task, of, pair)
        own_copy(task, of).start()

    chunk = min(128, rows)

    half_rows = rows // 2

    def factors(mb, of_core):
        def body(i, carry):
            at = pl.multiple_of(of_core * half_rows + i * chunk, chunk)
            row = lax.broadcasted_iota(jnp.int32, (chunk, rows), 0) + at
            col = lax.broadcasted_iota(jnp.int32, (chunk, rows), 1)
            peer = row // per_peer
            yc = (peer % group) * 2 + peer // group
            block = (row // PAD) % NZ
            slot = row % PAD
            rel = jnp.where(block % 2 == 1, NZ - (block + 1) // 2, block // 2)
            zz = (zi + rel) % NZ
            want = zz * (nyc * cap) + yc * cap + slot
            pick = jnp.where((col == want) & (slot < cap), 1.0, 0.0).astype(BF16)
            val = jnp.dot(pick, savedv[mb], preferred_element_type=F32)
            swapped = pltpu.roll(val, hidden, 1)
            is_gate = lax.broadcasted_iota(jnp.int32, (chunk, wide), 1) < hidden
            a = jnp.where(is_gate, val, swapped)
            u = jnp.where(is_gate, swapped, val)
            sg = jax.nn.sigmoid(a)
            silu = a * sg
            factor[mb, pl.ds(at, chunk), :] = jnp.where(
                is_gate, u * (sg * (1.0 + a * (1.0 - sg))), silu
            )
            act[pl.ds(mb * rows + at, chunk), :] = (silu * u)[:, : act.shape[1]].astype(BF16)
            return carry

        lax.fori_loop(0, half_rows // chunk, body, 0)

    def expert_stage(mb, of):
        at = pl.multiple_of(of * half_rows, half_rows)
        peers = pl.ds(of * group, group)
        grad = jnp.zeros((half_rows, wide), F32)
        for k in range(2):
            incoming = routed[mb, k, peers].reshape(half_rows, side)
            grad = grad + lax.dot_general(
                incoming,
                w2d[:, k * side : (k + 1) * side],
                (((1,), (1,)), ((), ())),
                preferred_element_type=F32,
            )
        out = (grad * factor[mb, pl.ds(at, half_rows), :]).astype(BF16)
        fog[mb, pl.ds(at, half_rows), :] = out
        for k in range(2):
            back = lax.dot_general(
                out,
                w1v[k * side : (k + 1) * side, :],
                (((1,), (1,)), ((), ())),
                preferred_element_type=F32,
            ).astype(BF16)
            rsend[mb, k, peers] = back.reshape(group, per_peer, side)
        for pair in (3, 2, 1, 0):
            own_return(mb, of, pair).start()
            for by in range(1, nyc):
                r_copy(mb, of, pair, (me + by) % nyc).start()

    def half_of(half):
        return slice(half * half_cols, (half + 1) * half_cols)

    def partial_of(of, at, half):
        return part[of, at // 2, (at % 2) * tok : (at % 2 + 1) * tok, half_of(half)]

    def sender(mb, of):
        def send(slot, extra=None):
            for half in SUMS[slot][1]:
                value = partial_of(of, SUMS[slot][2], half)
                if extra is not None:
                    value = value + sum_recv[mb, of, extra[0], :, half_of(half)].astype(F32)
                    if half in SUMS[extra[1]][1]:
                        value = value + sum_recv[mb, of, extra[1], :, half_of(half)].astype(F32)
                sum_send[mb, of, slot, :, half_of(half)] = value.astype(BF16)
                q_copy(mb, of, slot, half).start()

        def wait_sum(slot):
            if len(SUMS[slot][1]) == 2:
                wait_for(sum_recv.at[mb, of, slot], q_recv.at[mb, of, slot])
            else:
                half = SUMS[slot][1][0]
                cols = pl.ds(half * half_cols, half_cols)
                wait_for(sum_recv.at[mb, of, slot, :, cols], q_recv.at[mb, of, slot])

        return send, wait_sum

    def combine(mb, of):
        def partial_sums(pair):
            wait_for(rrecv.at[mb, of, pair], r_recv.at[mb, of, pair])
            back = rrecv[mb, of, pair].reshape(pair_rows, side)
            part[of, pair] = jnp.dot(comb[mb, of, pair], back, preferred_element_type=F32)

        send, _ = sender(mb, of)
        partial_sums(3)
        send(1)
        send(3)
        send(0)
        partial_sums(2)
        send(2)
        partial_sums(1)
        partial_sums(0)
        send(6)
        send(7)

    def hand_sums_on(mb, of):
        send, wait_sum = sender(mb, of)
        wait_sum(0)
        wait_sum(1)
        send(4, (0, 1))
        wait_sum(2)
        wait_sum(3)
        send(5, (2, 3))

    def stage_copy(mb):
        return pltpu.make_async_remote_copy(
            src_ref=gout.at[mb, other],
            dst_ref=stage.at[mb, core],
            send_sem=o_send.at[mb],
            recv_sem=o_recv.at[mb],
            device_id=along_y(sibling),
            device_id_type=MESH,
        )

    def finish(mb, of):
        for slot in (6, 7, 4, 5):
            wait_for(sum_recv.at[mb, of, slot], q_recv.at[mb, of, slot])
        total = gath[mb, of, 0, 0:tok, :].astype(F32) + part[of, 0, 0:tok, :]
        for slot in (6, 7, 4, 5):
            total = total + sum_recv[mb, of, slot].astype(F32)
        total = total.astype(BF16)
        gout[mb, of] = total

        @pl.when(pipe > 0)
        def _():
            spread_on(mb, of)

        @pl.when(of == core)
        def _():
            stage[mb, core] = total

        @pl.when(of != core)
        def _():
            stage_copy(mb).start()

    def turn_body(turn, carry):
        mb, of, is_chunk, is_gather, task, gather_of, back, end = plan(turn)

        @pl.when(is_gather)
        def _():
            gather(task, gather_of, is_chunk & jnp.logical_not(is_last))

        @pl.when(end[0] & jnp.logical_not((turn == 9) & (pipe == 0)))
        def _():
            finish(end[1], end[2])

        @pl.when(back[0])
        def _():
            combine(back[1], back[2])

        @pl.when(is_gather)
        def _():
            gather_rest(task, gather_of)

        @pl.when(is_last)
        def _():
            for at, chunks in ((5, ((1, 0),)), (6, ((1, 1),)), (8, ((2, 0), (2, 1))), (9, ((3, 0), (3, 1)))):

                @pl.when(turn == at)
                def _():
                    for chunk_at in chunks:
                        spread_own(*chunk_at)

        @pl.when(turn == 3)
        def _():
            for copy in weight_copies:
                copy.wait()

            @pl.when(jnp.logical_not(is_last))
            def _():
                def some_factors(some, carry):
                    factors(some // 2, some % 2)
                    return carry

                lax.fori_loop(0, 4, some_factors, 0)

        @pl.when(is_chunk)
        def _():
            @pl.when(is_last)
            def _():
                factors(mb, of)

            wait_rows(mb, of)
            expert_stage(mb, of)

        @pl.when(back[0])
        def _():
            hand_sums_on(back[1], back[2])

        return carry

    lax.fori_loop(0, 14, turn_body, 0)
    for task in (2, 3):
        for of in range(2):
            wait_rows(task, of)

    both_rows = 2 * rows
    tile = 256
    for start in range(0, hidden, tile):
        stop = min(start + tile, hidden)
        lanes = act[:, start : min(start + tile, act.shape[1])]
        for k in range(2):
            grads = routed[0:2, k].reshape(both_rows, side)
            g2 = lax.dot_general(lanes, grads, (((0,), (0,)), ((), ())), preferred_element_type=F32)
            g2_out[start:stop, k * side : (k + 1) * side] = g2[: stop - start].astype(BF16)
    outs = fog[...].reshape(both_rows, wide)

    def g1_body(i, carry):
        at = pl.multiple_of(i * tile, tile)
        col = pl.multiple_of((i % (side // tile)) * tile, tile)
        lanes = routed[2:4, i // (side // tile), :, :, pl.ds(col, tile)].reshape(both_rows, tile)
        g1 = lax.dot_general(lanes, outs, (((0,), (0,)), ((), ())), preferred_element_type=F32)
        g1_out[pl.ds(at, tile), :] = g1.astype(BF16)
        return carry

    lax.fori_loop(0, width // tile, g1_body, 0)

    @pl.when(pipe == 0)
    def _():
        finish(1, 1)

    for mb in range(2):
        stage_copy(mb).wait_recv()
        for k in range(2):
            sec_out[mb, :, k * side : (k + 1) * side] = stage[mb, k]

    def left(blocks, sem):
        wait_for(sendb.at[0, 0, pl.ds(0, blocks)], sem)

    wait_for(srecv.at[0, pl.ds(0, NZ - 1)], s_send.at[0])
    wait_for(srecv.at[0], s_send.at[1])
    for task in range(4):
        for of in range(2):
            left(3, f_send.at[task, of])
            left(nyc - 1, y_send.at[task, of])
            if task >= 2:
                left(4, d_send.at[task, of])
        if task >= 2:
            left(1, h_send.at[task])

    @pl.when(is_last)
    def _():
        for mb in range(2):
            left(1, h_send.at[mb])
            for of in range(2):
                left(4, d_send.at[mb, of])

    @pl.when(pipe > 0)
    def _():
        for mb in range(2):
            for of in range(2):
                left(5, e_send.at[mb, of])

    for mb in range(2):
        stage_copy(mb).wait_send()
        for of in range(2):
            left(7, q_send.at[mb, of])
            left(nyc - 1, r_send.at[mb, of])


def copy_kernel(parts, *refs):
    count = len(parts)
    in_sem, out_sem = refs[-2:]
    pairs = []
    for at in range(count):
        source, target, held = refs[at], refs[count + at], refs[2 * count + at]
        rows = source.shape[0] // parts[at]
        for piece in range(parts[at]):
            here = pl.ds(piece * rows, rows)
            no = len(pairs)
            pairs.append(
                (
                    pltpu.make_async_copy(source.at[here], held.at[here], in_sem.at[no]),
                    pltpu.make_async_copy(held.at[here], target.at[here], out_sem.at[no]),
                )
            )
    for bring, _ in pairs:
        bring.start()
    for bring, put in pairs:
        bring.wait()
        put.start()
    for _, put in pairs:
        put.wait()


def per_device(cotangent, expert_ids, gates, layer_inputs, saved_fc1, w_fc1, w_fc2):
    experts = lax.axis_size("expert")
    sections = lax.axis_size("pipe")
    nyc = experts // NZ
    micro, tok, width = cotangent.shape
    slots, wide = saved_fc1.shape[3:]
    hidden = wide // 2
    cap = slots // experts
    rows = experts * PAD
    per_peer = NZ * PAD
    side = width // 2
    dims = (sections, nyc, tok, width, wide, cap)
    vmem = pl.BlockSpec(memory_space=pltpu.VMEM)
    hbm = pl.BlockSpec(memory_space=pl.ANY)
    act_width = -(-hidden // 256) * 256
    dma = pltpu.SemaphoreType.DMA
    out = pl.pallas_call(
        functools.partial(fused_kernel, dims),
        out_shape=(
            jax.ShapeDtypeStruct((micro, tok, width), BF16),
            jax.ShapeDtypeStruct((width, wide), BF16),
            jax.ShapeDtypeStruct((hidden, width), BF16),
        ),
        in_specs=[vmem, vmem, vmem, vmem, hbm, hbm, hbm],
        out_specs=(vmem, vmem, vmem),
        scratch_shapes=[
            pltpu.VMEM((4, 2, NZ // 2, 2 * tok, side), BF16),
            pltpu.VMEM((4, 2, nyc, per_peer, side), BF16),
            pltpu.VMEM((4, 2, nyc, per_peer, side), BF16),
            pltpu.VMEM((2, 2, nyc, per_peer, side), BF16),
            pltpu.VMEM((2, 2, NZ // 2, nyc, 2 * PAD, side), BF16),
            pltpu.VMEM((2, NZ // 2, 2 * tok, side), F32),
            pltpu.VMEM((2, 2, 8, tok, side), BF16),
            pltpu.VMEM((2, 2, 8, tok, side), BF16),
            pltpu.VMEM((2, 2, tok, side), BF16),
            pltpu.VMEM((2, 2, tok, side), BF16),
            pltpu.VMEM((experts * PAD, 2 * tok), BF16),
            pltpu.VMEM((2, NZ, nyc * PAD, 2 * tok), BF16),
            pltpu.VMEM((4, 2, NZ // 2, 2 * nyc * PAD, 2 * tok), BF16),
            pltpu.VMEM((2, 2, NZ // 2, 2 * tok, 2 * nyc * PAD), BF16),
            pltpu.VMEM((width, wide), BF16),
            pltpu.VMEM((wide, width), BF16),
            pltpu.VMEM((2, rows, wide), BF16),
            pltpu.VMEM((2, rows, wide), F32),
            pltpu.VMEM((2 * rows, act_width), BF16),
            pltpu.VMEM((2, rows, wide), BF16),
            dma((4, 2)),
            dma((2, 2)),
            dma((4, 2)),
            dma((4, 2, 8, 2)),
            dma((4, 2)),
            dma((4, 2)),
            dma((2, 2)),
            dma((2, 2, 4)),
            dma((2, 2)),
            dma((2, 2, 8)),
            dma((2,)),
            dma(()),
            dma((2,)),
            dma((2,)),
            dma((4,)),
            dma((5,)),
        ],
        compiler_params=pltpu.CompilerParams(
            collective_id=0, has_side_effects=True, vmem_limit_bytes=60 * 1024 * 1024
        ),
        name="split_backward",
    )(
        cotangent,
        expert_ids[0].transpose(2, 0, 1),
        gates[0].transpose(2, 0, 1),
        layer_inputs[0],
        saved_fc1[0, :, 0],
        w_fc1[0, 0],
        w_fc2[0, 0],
    )
    parts = (2, 8, 4)
    out = pl.pallas_call(
        functools.partial(copy_kernel, parts),
        out_shape=tuple(jax.ShapeDtypeStruct(o.shape, o.dtype) for o in out),
        in_specs=[hbm] * 3,
        out_specs=(hbm,) * 3,
        scratch_shapes=[
            *(pltpu.VMEM(o.shape, o.dtype) for o in out),
            dma((sum(parts),)),
            dma((sum(parts),)),
        ],
        compiler_params=pltpu.CompilerParams(vmem_limit_bytes=60 * 1024 * 1024),
        name="copy_out",
    )(*out)
    return out[0][None], out[1][None, None], out[2][None, None]


def solution(mesh):
    in_specs = (
        P(None, "expert", None),
        P("pipe", None, "expert", None),
        P("pipe", None, "expert", None),
        P("pipe", None, "expert", None),
        P("pipe", None, "expert", None, None),
        P("pipe", "expert", None, None),
        P("pipe", "expert", None, None),
    )
    out_specs = (
        P("pipe", None, "expert", None),
        P("pipe", "expert", None, None),
        P("pipe", "expert", None, None),
    )
    return jax.shard_map(
        per_device, mesh=mesh, in_specs=in_specs, out_specs=out_specs, check_vma=False
    )
```

```python
import functools

import jax
import jax.numpy as jnp
from jax import lax
from jax.experimental import pallas as pl
from jax.experimental.pallas import tpu as pltpu
from jax.sharding import PartitionSpec as P

MESH = pl.DeviceIdType.MESH
NZ = 8
PAD = 8
F32, BF16 = jnp.float32, jnp.bfloat16


SUMS = {
    0: (1, (0, 1), 6),
    1: (2, (0,), 7),
    2: (-1, (0, 1), 5),
    3: (-2, (1,), 7),
    4: (2, (0, 1), 4),
    5: (-2, (0, 1), 3),
    6: (1, (0, 1), 2),
    7: (-1, (0, 1), 1),
}


def fused_kernel(
    dims,
    cot,
    ids,
    gates,
    xin,
    saved_hbm,
    w1_hbm,
    w2_hbm,
    sec_out,
    g1_out,
    g2_out,
    gath,
    sendb,
    routed,
    rsend,
    rrecv,
    part,
    sum_send,
    sum_recv,
    gout,
    stage,
    smat,
    srecv,
    sel,
    comb,
    w1v,
    w2d,
    savedv,
    factor,
    act,
    fog,
    d_send,
    e_send,
    f_send,
    z_recv,
    y_send,
    y_recv,
    r_send,
    r_recv,
    q_send,
    q_recv,
    s_send,
    s_recv,
    o_send,
    o_recv,
    h_send,
    local_sem,
):
    sections, nyc, tok, width, wide, cap = dims
    hidden = wide // 2
    side = width // 2
    half_cols = side // 2
    rows_in = NZ * nyc * cap
    rows = NZ * nyc * PAD
    per_peer = NZ * PAD
    pair_rows = 2 * nyc * PAD
    sel_rows = nyc * PAD
    group = nyc // 2

    pipe = lax.axis_index("pipe")
    expert = lax.axis_index("expert")
    zi = expert // nyc
    me = expert % nyc
    core = me % 2

    other = 1 - core
    sibling = me + 1 - 2 * core

    def along_z(by, plane=None, to=None):
        at = ((zi + by + NZ) % NZ) * nyc + (me if to is None else to)
        return (pipe if plane is None else plane, at)

    def along_y(yc):
        return (pipe, zi * nyc + yc)

    is_last = pipe == sections - 1
    before = (pipe + sections - 1) % sections
    after = (pipe + 1) % sections

    weight_copies = (
        pltpu.make_async_copy(w1_hbm, w1v, local_sem.at[0]),
        pltpu.make_async_copy(w2_hbm, w2d.at[pl.ds(0, hidden), :], local_sem.at[1]),
        pltpu.make_async_copy(w2_hbm, w2d.at[pl.ds(hidden, hidden), :], local_sem.at[2]),
        pltpu.make_async_copy(saved_hbm.at[0], savedv.at[0, pl.ds(0, rows_in), :], local_sem.at[3]),
        pltpu.make_async_copy(saved_hbm.at[1], savedv.at[1, pl.ds(0, rows_in), :], local_sem.at[4]),
    )

    barrier = pltpu.get_barrier_semaphore()
    for by in range(1, NZ):
        pl.semaphore_signal(barrier, inc=1, device_id=along_z(by), device_id_type=MESH)
        pl.semaphore_signal(
            barrier, inc=1, device_id=along_z(by, to=sibling), device_id_type=MESH
        )
    for by in range(1, nyc):
        pl.semaphore_signal(
            barrier, inc=1, device_id=along_y((me + by) % nyc), device_id_type=MESH
        )
    for by in range(-2, 3):
        for plane in (before, after):
            pl.semaphore_signal(
                barrier, inc=1, device_id=along_z(by, plane), device_id_type=MESH
            )

    for copy in weight_copies:
        copy.start()
    for mb in range(2):
        if rows > rows_in:
            savedv[mb, rows_in:rows, :] = jnp.zeros((rows - rows_in, wide), BF16)

    experts = NZ * nyc
    lanes_two = 2 * tok
    named = lax.broadcasted_iota(jnp.int32, (experts, lanes_two), 0)
    hit = jnp.zeros((experts, lanes_two), F32)
    weight = jnp.zeros((experts, lanes_two), F32)
    for k in range(ids.shape[0]):
        of_k = jnp.concatenate([ids[k, 0:1, :], ids[k, 1:2, :]], axis=1)
        gate_k = jnp.concatenate([gates[k, 0:1, :], gates[k, 1:2, :]], axis=1)
        same = named == of_k
        hit = hit + jnp.where(same, 1.0, 0.0)
        weight = weight + jnp.where(same, gate_k, 0.0)
    first = lax.broadcasted_iota(jnp.int32, (lanes_two, lanes_two), 0)
    second = lax.broadcasted_iota(jnp.int32, (lanes_two, lanes_two), 1)
    earlier = (first < second) & ((first < tok) == (second < tok))
    rank = jnp.dot(
        hit.astype(BF16),
        jnp.where(earlier, 1.0, 0.0).astype(BF16),
        preferred_element_type=F32,
    ).astype(jnp.int32)
    slot_no = lax.broadcasted_iota(jnp.int32, (experts, PAD, lanes_two), 1)
    spread_out = jnp.where(rank[:, None, :] == slot_no, weight[:, None, :], 0.0)
    smat[...] = spread_out.reshape(experts * PAD, lanes_two).astype(BF16)

    my_cols = pl.ds(pl.multiple_of(core * side, side), side)
    for mb in range(2):
        gath[2 + mb, core, 0, 0:tok, :] = xin[mb, :, my_cols]

    @pl.when(is_last)
    def _():
        for mb in range(2):
            gath[mb, core, 0, 0:tok, :] = cot[mb, :, my_cols]

    pltpu.make_async_copy(
        smat.at[pl.ds(pl.multiple_of(zi * sel_rows, sel_rows), sel_rows), :],
        srecv.at[core, 0],
        s_recv,
    ).start()
    pl.semaphore_wait(barrier, 2 * (NZ - 1) + nyc - 1 + 10)

    def wait_for(ref, sem):
        pltpu.make_async_copy(ref, ref, sem).wait()

    def selection_copy(by, swap):
        at = 0 if by == 0 else 2 * by - 1 if by <= 4 else 2 * (NZ - by)
        to = (zi + by) % NZ
        return pltpu.make_async_remote_copy(
            src_ref=smat.at[pl.ds(pl.multiple_of(to * sel_rows, sel_rows), sel_rows), :],
            dst_ref=srecv.at[core, at],
            send_sem=s_send.at[1 if swap else 0],
            recv_sem=s_recv,
            device_id=along_z(by, to=sibling if swap else me),
            device_id_type=MESH,
        )

    def block_view(task, of, at, half):
        return gath.at[
            task,
            of,
            at // 2,
            pl.ds((at % 2) * tok, tok),
            pl.ds(half * half_cols, half_cols),
        ]

    def spread_copy(src, task, of, by, at, half, sem, plane=None):
        return pltpu.make_async_remote_copy(
            src_ref=src,
            dst_ref=block_view(task, of, at, half),
            send_sem=sem,
            recv_sem=z_recv.at[task, of, at, half],
            device_id=along_z(by, plane),
            device_id_type=MESH,
        )

    def wait_block(task, of, at, half):
        wait_for(block_view(task, of, at, half), z_recv.at[task, of, at, half])

    def hand_over(source, mb, task):
        for half in range(2):
            at = pl.multiple_of(other * side + half * half_cols, half_cols)
            pltpu.make_async_remote_copy(
                src_ref=source.at[mb, :, pl.ds(at, half_cols)],
                dst_ref=block_view(task, core, 0, half),
                send_sem=h_send.at[task],
                recv_sem=z_recv.at[task, core, 0, half],
                device_id=along_y(sibling),
                device_id_type=MESH,
            ).start()

    def spread_own(task, of):
        @pl.when(other == of)
        def _():
            for half in range(2):
                wait_block(task, of, 0, half)

        for by, at in ((2, 3), (-2, 4), (1, 1), (-1, 2)):
            for half in range(2):
                src = block_view(task, of, 0, half)
                spread_copy(src, task, of, by, at, half, d_send.at[task, of]).start()

    def spread_on(mb, of):
        for by, at in ((2, 3), (-2, 4), (1, 1), (-1, 2), (0, 0)):
            for half in range(2):
                src = gout.at[mb, of, :, pl.ds(half * half_cols, half_cols)]
                spread_copy(src, mb, of, by, at, half, e_send.at[mb, of], before).start()

    def y_copy(task, of, by, at, count):
        to = (me + by) % nyc
        return pltpu.make_async_remote_copy(
            src_ref=sendb.at[task, of, to, pl.ds(at, count), :],
            dst_ref=routed.at[task, core, of * group + me // 2, pl.ds(at, count), :],
            send_sem=y_send.at[task, of],
            recv_sem=y_recv.at[task, of],
            device_id=along_y(to),
            device_id_type=MESH,
        )

    def own_copy(task, of):
        return pltpu.make_async_copy(
            sendb.at[task, of, me],
            routed.at[task, core, of * group + me // 2],
            y_recv.at[task, of],
        )

    def wait_rows(task, of):
        here = routed.at[task, :, pl.ds(of * group, group)]
        wait_for(here, y_recv.at[task, of])

    def r_copy(mb, of, pair, to):
        return pltpu.make_async_remote_copy(
            src_ref=rsend.at[mb, to % 2, of * group + to // 2, pl.ds(pair * 2 * PAD, 2 * PAD), :],
            dst_ref=rrecv.at[mb, of, pair, me],
            send_sem=r_send.at[mb, of],
            recv_sem=r_recv.at[mb, of, pair],
            device_id=along_y(to),
            device_id_type=MESH,
        )

    def own_return(mb, of, pair):
        return pltpu.make_async_copy(
            rsend.at[mb, core, of * group + me // 2, pl.ds(pair * 2 * PAD, 2 * PAD), :],
            rrecv.at[mb, of, pair, me],
            r_recv.at[mb, of, pair],
        )

    def q_copy(mb, of, slot, half):
        cols = pl.ds(half * half_cols, half_cols)
        return pltpu.make_async_remote_copy(
            src_ref=sum_send.at[mb, of, slot, :, cols],
            dst_ref=sum_recv.at[mb, of, slot, :, cols],
            send_sem=q_send.at[mb, of],
            recv_sem=q_recv.at[mb, of, slot],
            device_id=along_z(SUMS[slot][0]),
            device_id_type=MESH,
        )

    def plan(turn):
        chunk_no = turn - 4
        is_chunk = (turn >= 4) & (turn < 8)
        of = turn % 2
        mb = jnp.where(is_chunk, chunk_no // 2, 0)
        is_x = ((turn < 4) & jnp.logical_not(is_last)) | ((turn >= 10) & is_last)
        x_no = jnp.where(turn < 4, turn, turn - 10)
        task = jnp.where(is_chunk, mb, 2 + x_no // 2)
        gather_of = jnp.where(is_chunk, of, x_no % 2)
        is_back = (turn >= 5) & (turn <= 8)
        back_mb = jnp.where(is_back, (turn - 5) // 2, 0)
        is_end = (turn >= 6) & (turn <= 9)
        end_mb = jnp.where(is_end, (turn - 6) // 2, 0)
        back = (is_back, back_mb, (turn + 1) % 2)
        return mb, of, is_chunk, is_chunk | is_x, task, gather_of, back, (is_end, end_mb, of)

    @pl.when(is_last)
    def _():
        hand_over(cot, 0, 0)
        spread_own(0, 0)
        hand_over(cot, 1, 1)

    hand_over(xin, 0, 2)
    hand_over(xin, 1, 3)
    for by in range(NZ):
        for swap in (True, False):
            if by > 0 or swap:
                selection_copy(by, swap).start()

    @pl.when(jnp.logical_not(is_last))
    def _():
        for no in range(4):
            spread_own(2 + no // 2, no % 2)

    lane = lax.broadcasted_iota(jnp.int32, (sel_rows, 2 * tok), 1)
    low = lane < tok
    wait_for(srecv, s_recv)

    def build(of, carry):
        for pair in range(NZ // 2):
            first, second = srecv[of, 2 * pair].astype(F32), srecv[of, 2 * pair + 1].astype(F32)
            for mb in range(2):
                one = first if mb == 0 else pltpu.roll(first, tok, 1)
                two = second if mb == 1 else pltpu.roll(second, tok, 1)
                one = jnp.where(low, one, 0.0)
                two = jnp.where(low, 0.0, two)
                pieces = []
                for yc in range(nyc):
                    pieces += [one[yc * PAD : (yc + 1) * PAD], two[yc * PAD : (yc + 1) * PAD]]
                both = jnp.concatenate(pieces, axis=0)
                ones = jnp.where(both != 0.0, 1.0, 0.0)
                sel[mb, of, pair] = both.astype(BF16)
                sel[2 + mb, of, pair] = ones.astype(BF16)
                comb[mb, of, pair] = ones.T.astype(BF16)
        return carry

    lax.fori_loop(0, 2, build, 0)

    @pl.when(is_last)
    def _():
        spread_own(0, 1)

    def select(task, of, pair):
        chosen = jnp.dot(
            sel[task, of, pair], gath[task, of, pair], preferred_element_type=F32
        ).astype(BF16)
        at = pair * 2 * PAD
        for yc in range(nyc):
            sendb[task, of, yc, at : at + 2 * PAD, :] = chosen[yc * 2 * PAD : (yc + 1) * 2 * PAD]
        for by in range(1, nyc):
            y_copy(task, of, by, at, 2 * PAD).start()

    def gather(task, of, is_handed_on):
        def forward(from_at, by, at, half):
            src = block_view(task, of, from_at, half)
            spread_copy(src, task, of, by, at, half, f_send.at[task, of]).start()

        wait_block(task, of, 3, 0)
        forward(3, 2, 7, 0)
        forward(3, 1, 5, 0)
        wait_block(task, of, 4, 1)
        forward(4, -2, 7, 1)
        forward(4, -1, 6, 1)
        wait_block(task, of, 3, 1)
        forward(3, 1, 5, 1)
        wait_block(task, of, 4, 0)
        forward(4, -1, 6, 0)
        for half in range(2):
            wait_block(task, of, 1, half)

        @pl.when(is_handed_on)
        def _():
            for half in range(2):
                wait_block(task, of, 0, half)

        select(task, of, 0)
        for half in range(2):
            wait_block(task, of, 2, half)
        select(task, of, 1)

    def gather_rest(task, of):
        for pair, needs in ((2, (5,)), (3, (6, 7))):
            for at in needs:
                for half in range(2):
                    wait_block(task, of, at, half)
            select(task, of, pair)
        own_copy(task, of).start()

    chunk = min(128, rows)

    half_rows = rows // 2

    def factors(mb, of_core):
        def body(i, carry):
            at = pl.multiple_of(of_core * half_rows + i * chunk, chunk)
            row = lax.broadcasted_iota(jnp.int32, (chunk, rows), 0) + at
            col = lax.broadcasted_iota(jnp.int32, (chunk, rows), 1)
            peer = row // per_peer
            yc = (peer % group) * 2 + peer // group
            block = (row // PAD) % NZ
            slot = row % PAD
            rel = jnp.where(block % 2 == 1, NZ - (block + 1) // 2, block // 2)
            zz = (zi + rel) % NZ
            want = zz * (nyc * cap) + yc * cap + slot
            pick = jnp.where((col == want) & (slot < cap), 1.0, 0.0).astype(BF16)
            val = jnp.dot(pick, savedv[mb], preferred_element_type=F32)
            swapped = pltpu.roll(val, hidden, 1)
            is_gate = lax.broadcasted_iota(jnp.int32, (chunk, wide), 1) < hidden
            a = jnp.where(is_gate, val, swapped)
            u = jnp.where(is_gate, swapped, val)
            sg = jax.nn.sigmoid(a)
            silu = a * sg
            factor[mb, pl.ds(at, chunk), :] = jnp.where(
                is_gate, u * (sg * (1.0 + a * (1.0 - sg))), silu
            )
            act[pl.ds(mb * rows + at, chunk), :] = (silu * u)[:, : act.shape[1]].astype(BF16)
            return carry

        lax.fori_loop(0, half_rows // chunk, body, 0)

    def expert_stage(mb, of):
        at = pl.multiple_of(of * half_rows, half_rows)
        peers = pl.ds(of * group, group)
        grad = jnp.zeros((half_rows, wide), F32)
        for k in range(2):
            incoming = routed[mb, k, peers].reshape(half_rows, side)
            grad = grad + lax.dot_general(
                incoming,
                w2d[:, k * side : (k + 1) * side],
                (((1,), (1,)), ((), ())),
                preferred_element_type=F32,
            )
        out = (grad * factor[mb, pl.ds(at, half_rows), :]).astype(BF16)
        fog[mb, pl.ds(at, half_rows), :] = out
        for k in range(2):
            back = lax.dot_general(
                out,
                w1v[k * side : (k + 1) * side, :],
                (((1,), (1,)), ((), ())),
                preferred_element_type=F32,
            ).astype(BF16)
            rsend[mb, k, peers] = back.reshape(group, per_peer, side)
        for pair in (3, 2, 1, 0):
            own_return(mb, of, pair).start()
            for by in range(1, nyc):
                r_copy(mb, of, pair, (me + by) % nyc).start()

    def half_of(half):
        return slice(half * half_cols, (half + 1) * half_cols)

    def partial_of(of, at, half):
        return part[of, at // 2, (at % 2) * tok : (at % 2 + 1) * tok, half_of(half)]

    def sender(mb, of):
        def send(slot, extra=None):
            for half in SUMS[slot][1]:
                value = partial_of(of, SUMS[slot][2], half)
                if extra is not None:
                    value = value + sum_recv[mb, of, extra[0], :, half_of(half)].astype(F32)
                    if half in SUMS[extra[1]][1]:
                        value = value + sum_recv[mb, of, extra[1], :, half_of(half)].astype(F32)
                sum_send[mb, of, slot, :, half_of(half)] = value.astype(BF16)
                q_copy(mb, of, slot, half).start()

        def wait_sum(slot):
            if len(SUMS[slot][1]) == 2:
                wait_for(sum_recv.at[mb, of, slot], q_recv.at[mb, of, slot])
            else:
                half = SUMS[slot][1][0]
                cols = pl.ds(half * half_cols, half_cols)
                wait_for(sum_recv.at[mb, of, slot, :, cols], q_recv.at[mb, of, slot])

        return send, wait_sum

    def combine(mb, of):
        def partial_sums(pair):
            wait_for(rrecv.at[mb, of, pair], r_recv.at[mb, of, pair])
            back = rrecv[mb, of, pair].reshape(pair_rows, side)
            part[of, pair] = jnp.dot(comb[mb, of, pair], back, preferred_element_type=F32)

        send, _ = sender(mb, of)
        partial_sums(3)
        send(1)
        send(3)
        send(0)
        partial_sums(2)
        send(2)
        partial_sums(1)
        partial_sums(0)
        send(6)
        send(7)

    def hand_sums_on(mb, of):
        send, wait_sum = sender(mb, of)
        wait_sum(0)
        wait_sum(1)
        send(4, (0, 1))
        wait_sum(2)
        wait_sum(3)
        send(5, (2, 3))

    def stage_copy(mb):
        return pltpu.make_async_remote_copy(
            src_ref=gout.at[mb, other],
            dst_ref=stage.at[mb, core],
            send_sem=o_send.at[mb],
            recv_sem=o_recv.at[mb],
            device_id=along_y(sibling),
            device_id_type=MESH,
        )

    def finish(mb, of):
        for slot in (6, 7, 4, 5):
            wait_for(sum_recv.at[mb, of, slot], q_recv.at[mb, of, slot])
        total = gath[mb, of, 0, 0:tok, :].astype(F32) + part[of, 0, 0:tok, :]
        for slot in (6, 7, 4, 5):
            total = total + sum_recv[mb, of, slot].astype(F32)
        total = total.astype(BF16)
        gout[mb, of] = total

        @pl.when(pipe > 0)
        def _():
            spread_on(mb, of)

        @pl.when(of == core)
        def _():
            stage[mb, core] = total

        @pl.when(of != core)
        def _():
            stage_copy(mb).start()

    def turn_body(turn, carry):
        mb, of, is_chunk, is_gather, task, gather_of, back, end = plan(turn)

        @pl.when(is_gather)
        def _():
            gather(task, gather_of, is_chunk & jnp.logical_not(is_last))

        @pl.when(end[0] & jnp.logical_not((turn == 9) & (pipe == 0)))
        def _():
            finish(end[1], end[2])

        @pl.when(back[0])
        def _():
            combine(back[1], back[2])

        @pl.when(is_gather)
        def _():
            gather_rest(task, gather_of)

        @pl.when(back[0])
        def _():
            hand_sums_on(back[1], back[2])

        @pl.when(is_last)
        def _():
            for at, chunks in ((5, ((1, 0),)), (6, ((1, 1),)), (8, ((2, 0), (2, 1))), (9, ((3, 0), (3, 1)))):

                @pl.when(turn == at)
                def _():
                    for chunk_at in chunks:
                        spread_own(*chunk_at)

        @pl.when(turn == 3)
        def _():
            for copy in weight_copies:
                copy.wait()

            @pl.when(jnp.logical_not(is_last))
            def _():
                def some_factors(some, carry):
                    factors(some // 2, some % 2)
                    return carry

                lax.fori_loop(0, 4, some_factors, 0)

        @pl.when(is_chunk)
        def _():
            @pl.when(is_last)
            def _():
                factors(mb, of)

            wait_rows(mb, of)
            expert_stage(mb, of)

        return carry

    lax.fori_loop(0, 14, turn_body, 0)
    for task in (2, 3):
        for of in range(2):
            wait_rows(task, of)

    both_rows = 2 * rows
    tile = 256
    for start in range(0, hidden, tile):
        stop = min(start + tile, hidden)
        lanes = act[:, start : min(start + tile, act.shape[1])]
        for k in range(2):
            grads = routed[0:2, k].reshape(both_rows, side)
            g2 = lax.dot_general(lanes, grads, (((0,), (0,)), ((), ())), preferred_element_type=F32)
            g2_out[start:stop, k * side : (k + 1) * side] = g2[: stop - start].astype(BF16)
    outs = fog[...].reshape(both_rows, wide)

    def g1_body(i, carry):
        at = pl.multiple_of(i * tile, tile)
        col = pl.multiple_of((i % (side // tile)) * tile, tile)
        lanes = routed[2:4, i // (side // tile), :, :, pl.ds(col, tile)].reshape(both_rows, tile)
        g1 = lax.dot_general(lanes, outs, (((0,), (0,)), ((), ())), preferred_element_type=F32)
        g1_out[pl.ds(at, tile), :] = g1.astype(BF16)
        return carry

    lax.fori_loop(0, width // tile, g1_body, 0)

    @pl.when(pipe == 0)
    def _():
        finish(1, 1)

    for mb in range(2):
        stage_copy(mb).wait_recv()
        for k in range(2):
            sec_out[mb, :, k * side : (k + 1) * side] = stage[mb, k]

    def left(blocks, sem):
        wait_for(sendb.at[0, 0, pl.ds(0, blocks)], sem)

    wait_for(srecv.at[0, pl.ds(0, NZ - 1)], s_send.at[0])
    wait_for(srecv.at[0], s_send.at[1])
    for task in range(4):
        for of in range(2):
            left(3, f_send.at[task, of])
            left(nyc - 1, y_send.at[task, of])
            if task >= 2:
                left(4, d_send.at[task, of])
        if task >= 2:
            left(1, h_send.at[task])

    @pl.when(is_last)
    def _():
        for mb in range(2):
            left(1, h_send.at[mb])
            for of in range(2):
                left(4, d_send.at[mb, of])

    @pl.when(pipe > 0)
    def _():
        for mb in range(2):
            for of in range(2):
                left(5, e_send.at[mb, of])

    for mb in range(2):
        stage_copy(mb).wait_send()
        for of in range(2):
            left(7, q_send.at[mb, of])
            left(nyc - 1, r_send.at[mb, of])


def copy_kernel(parts, *refs):
    count = len(parts)
    in_sem, out_sem = refs[-2:]
    pairs = []
    for at in range(count):
        source, target, held = refs[at], refs[count + at], refs[2 * count + at]
        rows = source.shape[0] // parts[at]
        for piece in range(parts[at]):
            here = pl.ds(piece * rows, rows)
            no = len(pairs)
            pairs.append(
                (
                    pltpu.make_async_copy(source.at[here], held.at[here], in_sem.at[no]),
                    pltpu.make_async_copy(held.at[here], target.at[here], out_sem.at[no]),
                )
            )
    for bring, _ in pairs:
        bring.start()
    for bring, put in pairs:
        bring.wait()
        put.start()
    for _, put in pairs:
        put.wait()


def per_device(cotangent, expert_ids, gates, layer_inputs, saved_fc1, w_fc1, w_fc2):
    experts = lax.axis_size("expert")
    sections = lax.axis_size("pipe")
    nyc = experts // NZ
    micro, tok, width = cotangent.shape
    slots, wide = saved_fc1.shape[3:]
    hidden = wide // 2
    cap = slots // experts
    rows = experts * PAD
    per_peer = NZ * PAD
    side = width // 2
    dims = (sections, nyc, tok, width, wide, cap)
    vmem = pl.BlockSpec(memory_space=pltpu.VMEM)
    hbm = pl.BlockSpec(memory_space=pl.ANY)
    act_width = -(-hidden // 256) * 256
    dma = pltpu.SemaphoreType.DMA
    out = pl.pallas_call(
        functools.partial(fused_kernel, dims),
        out_shape=(
            jax.ShapeDtypeStruct((micro, tok, width), BF16),
            jax.ShapeDtypeStruct((width, wide), BF16),
            jax.ShapeDtypeStruct((hidden, width), BF16),
        ),
        in_specs=[vmem, vmem, vmem, vmem, hbm, hbm, hbm],
        out_specs=(vmem, vmem, vmem),
        scratch_shapes=[
            pltpu.VMEM((4, 2, NZ // 2, 2 * tok, side), BF16),
            pltpu.VMEM((4, 2, nyc, per_peer, side), BF16),
            pltpu.VMEM((4, 2, nyc, per_peer, side), BF16),
            pltpu.VMEM((2, 2, nyc, per_peer, side), BF16),
            pltpu.VMEM((2, 2, NZ // 2, nyc, 2 * PAD, side), BF16),
            pltpu.VMEM((2, NZ // 2, 2 * tok, side), F32),
            pltpu.VMEM((2, 2, 8, tok, side), BF16),
            pltpu.VMEM((2, 2, 8, tok, side), BF16),
            pltpu.VMEM((2, 2, tok, side), BF16),
            pltpu.VMEM((2, 2, tok, side), BF16),
            pltpu.VMEM((experts * PAD, 2 * tok), BF16),
            pltpu.VMEM((2, NZ, nyc * PAD, 2 * tok), BF16),
            pltpu.VMEM((4, 2, NZ // 2, 2 * nyc * PAD, 2 * tok), BF16),
            pltpu.VMEM((2, 2, NZ // 2, 2 * tok, 2 * nyc * PAD), BF16),
            pltpu.VMEM((width, wide), BF16),
            pltpu.VMEM((wide, width), BF16),
            pltpu.VMEM((2, rows, wide), BF16),
            pltpu.VMEM((2, rows, wide), F32),
            pltpu.VMEM((2 * rows, act_width), BF16),
            pltpu.VMEM((2, rows, wide), BF16),
            dma((4, 2)),
            dma((2, 2)),
            dma((4, 2)),
            dma((4, 2, 8, 2)),
            dma((4, 2)),
            dma((4, 2)),
            dma((2, 2)),
            dma((2, 2, 4)),
            dma((2, 2)),
            dma((2, 2, 8)),
            dma((2,)),
            dma(()),
            dma((2,)),
            dma((2,)),
            dma((4,)),
            dma((5,)),
        ],
        compiler_params=pltpu.CompilerParams(
            collective_id=0, has_side_effects=True, vmem_limit_bytes=60 * 1024 * 1024
        ),
        name="split_backward",
    )(
        cotangent,
        expert_ids[0].transpose(2, 0, 1),
        gates[0].transpose(2, 0, 1),
        layer_inputs[0],
        saved_fc1[0, :, 0],
        w_fc1[0, 0],
        w_fc2[0, 0],
    )
    parts = (2, 8, 4)
    out = pl.pallas_call(
        functools.partial(copy_kernel, parts),
        out_shape=tuple(jax.ShapeDtypeStruct(o.shape, o.dtype) for o in out),
        in_specs=[hbm] * 3,
        out_specs=(hbm,) * 3,
        scratch_shapes=[
            *(pltpu.VMEM(o.shape, o.dtype) for o in out),
            dma((sum(parts),)),
            dma((sum(parts),)),
        ],
        compiler_params=pltpu.CompilerParams(vmem_limit_bytes=60 * 1024 * 1024),
        name="copy_out",
    )(*out)
    return out[0][None], out[1][None, None], out[2][None, None]


def solution(mesh):
    in_specs = (
        P(None, "expert", None),
        P("pipe", None, "expert", None),
        P("pipe", None, "expert", None),
        P("pipe", None, "expert", None),
        P("pipe", None, "expert", None, None),
        P("pipe", "expert", None, None),
        P("pipe", "expert", None, None),
    )
    out_specs = (
        P("pipe", None, "expert", None),
        P("pipe", "expert", None, None),
        P("pipe", "expert", None, None),
    )
    return jax.shard_map(
        per_device, mesh=mesh, in_specs=in_specs, out_specs=out_specs, check_vma=False
    )
```
